32 devices in a mesh: rep: 16 (over z, x, core), grp: 2 (over y).
Axes of the slice: x: 2, y: 2, z: 4, core: 2. Of those that a mesh axis runs over, the one named last changes fastest.
Arguments:
- tokens: bfloat16 [16, 1024, 768], P('rep', 'grp'), may hold values from -6 to 6
- segment_ids: int32 [16, 1024], P('rep', 'grp'), may hold values from 0 to 2, as said below
- expert_ids: int32 [16, 1024, 1], P('rep', 'grp'), may hold values from 0 to 7; in each aligned block of 512 rows (0 to 511, 512 to 1023, ..., all dimensions but the last counted through in order) at most 128 rows name the same one
- rel_bucket: int32 [2047], replicated, may hold values from 0 to 31
- query_key_value_weight: bfloat16 [768, 2304], P('grp'), may hold values from -0.21875 to 0.21875
- output_weight: bfloat16 [768, 768], P('grp'), may hold values from -1.75 to 1.75
- router_weight: bfloat16 [768, 8], P('grp'), may hold values from -0.21875 to 0.21875
- gain_attn: bfloat16 [768], P('grp'), may hold values from 0.5 to 1.5
- gain_ffn: bfloat16 [768], P('grp'), may hold values from 0.5 to 1.5
- rel_table: bfloat16 [32, 12], P('grp'), may hold values from -4 to 4
- w_up: bfloat16 [24576, 768], P('grp'), may hold values from -0.21875 to 0.21875
- w_down: bfloat16 [24576, 768], P('grp'), may hold values from -1.25 to 1.25
- out_grad: bfloat16 [16, 1024, 768], P('rep', 'grp'), may hold values from -6 to 6
Outputs:
- layer_out: bfloat16 [16, 1024, 768], P('rep', 'grp')
- tokens_grad: float32 [16, 1024, 768], P('rep', 'grp')
- grad_w_qkv: float32 [768, 2304], P('grp')
- grad_w_out: float32 [768, 768], P('grp')
- grad_w_router: float32 [768, 8], P('grp')
- grad_gain_attn: float32 [768], P('grp')
- grad_gain_ffn: float32 [768], P('grp')
- grad_rel_table: float32 [32, 12], P('grp')
- grad_w_up: float32 [24576, 768], P('grp')
- grad_w_down: float32 [24576, 768], P('grp')
The draws below stay inside these ranges and needn't reach their ends.
Inputs may be any that keep to these rules, and one draw needn't show every extreme that they name: `segment_ids`: ids never fall along a sequence. `expert_ids`: in each aligned block of 512 positions of a sequence at most 128 tokens name one expert.
All inputs are finite; a program needn't handle non-finite values.
Results may differ from the reference program's by a relative error of at most 0.025.
Values may be sent and summed in bfloat16 or wider, within the bound.
No kernel may reach another device: no remote copies, remote signals or barrier semaphores. Data moves between devices by JAX's collectives and lax.ppermute only.
A program may use at most 512 MiB of HBM per device.

```python
import math
import jax
import jax.numpy as jnp
import numpy as np
from jax import lax

D = 768
HEADS = 12
HEAD_DIM = 64
FF = 3072
BUCKETS = 32
EXPERTS = 8
SEQ_LEN = 1024
SEQS = 1
BATCH = 16
SPAN = 512
MOST = 128
N_GRP = 2


def draw_segment_ids(key, part):
    key = jax.random.fold_in(key, 7)
    key_cut, key_on, key_pick, key_lo, key_hi = jax.random.split(key, 5)
    one_third = SEQ_LEN // 3
    jitter = max(SEQ_LEN // 12, 1)
    cut_points = one_third * jnp.arange(1, 3, dtype=jnp.int32)[None, :] + jax.random.randint(key_cut, (BATCH, 2), -jitter, jitter + 1)
    active = jax.random.randint(key_on, (BATCH, 2), 0, 2)
    chosen = jax.random.randint(key_pick, (BATCH // SEQS,), 0, SEQS)
    marked = jnp.arange(BATCH) % SEQS == jnp.repeat(chosen, SEQS)
    low_cut = jax.random.randint(key_lo, (BATCH,), 1, SPAN)
    high_cut = jax.random.randint(key_hi, (BATCH,), SEQ_LEN - SPAN + 1, SEQ_LEN)
    edge_cuts = jnp.stack([low_cut, high_cut], axis=1)
    cut_points = jnp.where(marked[:, None], edge_cuts, cut_points)
    active = jnp.where(marked[:, None], 1, active)
    position = jnp.arange(SEQ_LEN, dtype=jnp.int32)
    passed = (position[None, None, :] >= cut_points[:, :, None]).astype(jnp.int32)
    return jnp.sum(active[:, :, None] * passed, axis=1).astype(jnp.int32)


def place_ends(values, rng, smallest, high):
    dims = values.shape
    place = [jax.random.randint(jax.random.fold_in(rng, axis), (), 0, dims[axis]) for axis in range(len(dims))]
    values = values.at[tuple(place)].set(smallest)
    longest = dims.index(max(dims))
    place[longest] = (place[longest] + 1) % dims[longest]
    return values.at[tuple(place)].set(high)


def levels(stream_key, extent, shards, smallest, high):
    gain, own = 1.0, jax.random.fold_in(stream_key, 6)
    for dim, parts in shards:
        draws = jnp.exp(jax.random.uniform(jax.random.fold_in(own, dim), (parts,), jnp.float32, smallest / len(shards), high / len(shards)))
        gain = gain * jnp.repeat(draws, extent[dim] // parts).reshape([-1 if axis == dim else 1 for axis in range(len(extent))])
    return gain


def assign_block(stream_key, own, number, rows, amount, top, most, lean):
    order = jax.random.permutation(stream_key, amount)
    packed, common = shares(amount, rows * top, most, lean, True), shares(amount, rows * top, most, lean, False)
    places = jnp.arange(amount)

    def named(tallies, turn):
        used = int((tallies > 0).sum())
        fixed = max(1, used // 4)
        moved = fixed + (places - fixed + turn * (used - fixed)) % max(1, amount - fixed)
        return jnp.zeros((amount,), jnp.int32).at[order[jnp.where(places < fixed, places, moved)]].set(jnp.asarray(tallies, jnp.int32))

    tallies = jnp.where(number % 4 == 0, named(packed, number // 4), named(common, number - number // 4 - 1))
    mixed = jax.random.permutation(jax.random.fold_in(own, 3), amount)
    donor, receiver = mixed[0:amount // 2 * 2:2], mixed[1:amount // 2 * 2:2]
    slack = jnp.minimum(tallies[donor] - 1, most - tallies[receiver]) // 2
    slack = jnp.where((donor == order[0]) | (receiver == order[0]) | (tallies[receiver] == 0), 0, jnp.maximum(slack, 0))
    moved = jax.random.randint(jax.random.fold_in(own, 4), (amount // 2,), 0, 1 << 20) % (slack + 1)
    tallies = tallies.at[donor].add(-moved).at[receiver].add(moved)
    items = jnp.searchsorted(jnp.cumsum(tallies), jnp.arange(rows * top), side="right").astype(jnp.int32)
    listing = items.reshape(top, rows).T
    listing = listing[jax.random.permutation(jax.random.fold_in(own, 1), rows)]
    turn = jax.random.randint(jax.random.fold_in(own, 2), (rows, 1), 0, top)
    return jnp.take_along_axis(listing, (jnp.arange(top)[None, :] + turn) % top, axis=1)


def shares(number_of, total, bound, slope, full):
    weights = [(1 << 20) // math.isqrt(grade ** slope) + 1 for grade in range(1, number_of + 1)]
    largest = bound if full else min(bound, max(-(-total // number_of), total * weights[0] // sum(weights)))
    least = 1 if total - largest >= number_of - 1 else 0
    holding, rest = [largest] + [least] * (number_of - 1), total - largest - least * (number_of - 1)
    while rest > 0:
        free = [i for i in range(1, number_of) if holding[i] < largest] or [i for i in range(1, number_of) if holding[i] < bound]
        pool, budget = sum([weights[i] for i in free]), rest
        for i in free:
            more = min(bound - holding[i], max(1, budget * weights[i] // pool), rest)
            holding[i] = holding[i] + more
            rest = rest - more
    return np.array(holding)


def gaussian(key, extent, deviation, most, cuts=(), kind=jnp.bfloat16):
    loudness = levels(key, extent, cuts, -0.22, 0.18) if cuts else 1.0
    array = jax.random.normal(key, extent, jnp.float32) * deviation * loudness
    return jnp.minimum(jnp.maximum(array, -most), most).astype(kind)


def setup_inputs(seed: int = 0) -> dict:
    key_list = jax.random.split(jax.random.key(seed), 14)
    tokens = gaussian(key_list[0], (BATCH, SEQ_LEN, D), 1.0, 6.0, ((0, 16), (1, 2)))
    segment_ids = draw_segment_ids(jax.random.fold_in(key_list[13], 71), 0)
    expert_ids_keys = jax.random.split(jax.random.fold_in(key_list[2], 1), BATCH * SEQ_LEN // SPAN)
    expert_ids_turns = jax.random.permutation(jax.random.fold_in(key_list[2], 3), BATCH * SEQ_LEN // SPAN)
    expert_ids = jax.vmap(lambda own, number: assign_block(jax.random.fold_in(key_list[2], 2), own, number, SPAN, EXPERTS, 1, MOST, 1))(expert_ids_keys, expert_ids_turns).reshape((BATCH, SEQ_LEN, 1))
    rel_bucket = place_ends(jax.random.randint(key_list[3], (2 * SEQ_LEN - 1,), 0, BUCKETS), jax.random.fold_in(key_list[3], 1), 0, BUCKETS - 1).astype(jnp.int32)
    query_key_value_weight = gaussian(key_list[4], (D, 3 * D), D ** -0.5, 0.21875, ((0, 2),))
    output_weight = gaussian(key_list[5], (D, D), (max(D // 64, 1)) ** -0.5, 1.75, ((0, 2),))
    router_weight = gaussian(key_list[6], (D, EXPERTS), D ** -0.5, 0.21875, ((0, 2),))
    gain_attn = jnp.clip(1.0 + 0.1 * jax.random.normal(key_list[7], (D,), jnp.float32), 0.5, 1.5).astype(jnp.bfloat16)
    gain_ffn = jnp.clip(1.0 + 0.1 * jax.random.normal(key_list[8], (D,), jnp.float32), 0.5, 1.5).astype(jnp.bfloat16)
    rel_table = gaussian(key_list[9], (BUCKETS, HEADS), 1.0, 4.0, ((0, 2),))
    w_up = gaussian(key_list[10], (EXPERTS * FF, D), D ** -0.5, 0.21875, ((0, 2),))
    w_down = gaussian(key_list[11], (EXPERTS * FF, D), (max(FF // 128, 1)) ** -0.5, 1.25, ((0, 2),))
    out_grad = gaussian(key_list[12], (BATCH, SEQ_LEN, D), 1.0, 6.0, ((0, 16), (1, 2)))
    return {"tokens": tokens, "segment_ids": segment_ids, "expert_ids": expert_ids, "rel_bucket": rel_bucket, "query_key_value_weight": query_key_value_weight, "output_weight": output_weight, "router_weight": router_weight, "gain_attn": gain_attn, "gain_ffn": gain_ffn, "rel_table": rel_table, "w_up": w_up, "w_down": w_down, "out_grad": out_grad}


@jax.custom_vjp
def low(v):
    return lax.optimization_barrier(v.astype(jnp.bfloat16)).astype(jnp.float32)

@jax.custom_vjp
def low_back(v):
    return v

def low_keep(v):
    return (low(v), None)

def low_pass(kept, grad):
    return (grad,)

def back_keep(v):
    return (v, None)

def back_low(kept, grad):
    return (low(grad),)
low.defvjp(low_keep, low_pass)
low_back.defvjp(back_keep, back_low)
eps_norm = 1e-06
neg_fill = -1e+30
highest_precision = lax.Precision.HIGHEST

def rms_scale(values, gain_vec):
    inverse = lax.rsqrt(lax.optimization_barrier(jnp.mean(values * values, axis=-1, keepdims=True)) + eps_norm)
    return values * inverse * gain_vec

def attend_one(pieces, pos_bias):
    query_heads, key_heads, value_heads, seg_ids = pieces
    scores = jnp.einsum('qhd,khd->hqk', query_heads, key_heads, precision=highest_precision) * HEAD_DIM ** (-0.5) + pos_bias
    scores = low_back(scores)
    same_doc = seg_ids[:, None] == seg_ids[None, :]
    scores = jnp.where(same_doc[None], scores, neg_fill)
    row_max = lax.optimization_barrier(jnp.max(scores, axis=-1, keepdims=True))
    log_total = row_max + jnp.log(lax.optimization_barrier(jnp.sum(jnp.exp(scores - row_max), axis=-1, keepdims=True)))
    attn_probs = low(jnp.exp(scores - log_total))
    return jnp.einsum('hqk,khd->qhd', attn_probs, value_heads, precision=highest_precision)

def forward(input_tokens, seg_ids, expert_index, rel_bucket, query_key_value_weight, output_weight, router_weight, gain_attn, gain_ffn, rel_table, w_up, w_down):
    normalized_input = low(rms_scale(input_tokens, gain_attn))
    projected_output = jnp.einsum('mkw,wy->mky', normalized_input, query_key_value_weight, precision=highest_precision)

    def shaped(column_part):
        return low(low_back(column_part)).reshape(SEQS, SEQ_LEN, HEADS, HEAD_DIM)
    query_heads = shaped(projected_output[..., :D])
    key_heads = shaped(projected_output[..., D:2 * D])
    value_heads = shaped(projected_output[..., 2 * D:])
    offsets = jnp.arange(SEQ_LEN)[None, :] - jnp.arange(SEQ_LEN)[:, None] + SEQ_LEN - 1
    pos_bias = jnp.transpose(rel_table[rel_bucket[offsets]], (2, 0, 1))
    attention_result = lax.map(jax.checkpoint(lambda pieces: attend_one(pieces, pos_bias)), (query_heads, key_heads, value_heads, seg_ids))
    attention_result = low(low_back(attention_result.reshape(SEQS, SEQ_LEN, D)))
    residual_stream = input_tokens + low_back(jnp.einsum('mkw,wy->mky', attention_result, output_weight, precision=highest_precision))
    normalized_feedforward = low(rms_scale(residual_stream, gain_ffn))
    router_logits = low_back(jnp.einsum('mkw,wy->mky', normalized_feedforward, router_weight, precision=highest_precision))
    router = jax.nn.softmax(router_logits, axis=-1)
    chosen = (expert_index[..., None] == jnp.arange(EXPERTS)).astype(jnp.int32)
    gate_prob = lax.optimization_barrier(jnp.sum(router * chosen, axis=-1))
    blocks = chosen.reshape(SEQS, N_GRP, SPAN, EXPERTS)
    slot_rank = lax.optimization_barrier(jnp.sum((jnp.cumsum(blocks, axis=2) - blocks) * blocks, axis=-1))
    slot_index = lax.optimization_barrier(jnp.sum(blocks * jnp.arange(EXPERTS), axis=-1)) * MOST + slot_rank
    dispatch = (slot_index[..., None] == jnp.arange(EXPERTS * MOST)).astype(jnp.float32)
    token_rows = normalized_feedforward.reshape(SEQS, N_GRP, SPAN, D)
    expert_in = low_back(jnp.einsum('sgtc,sgtd->sgcd', dispatch, token_rows, precision=highest_precision))
    expert_in = expert_in.reshape(SEQS, N_GRP, EXPERTS, MOST, D)
    up_rows = w_up.reshape(EXPERTS, FF, D)
    down_rows = w_down.reshape(EXPERTS, FF, D)
    pre_act = low_back(jnp.einsum('sgemd,efd->sgemf', expert_in, up_rows, precision=highest_precision))
    activated = low(jax.nn.gelu(pre_act, approximate=True))
    expert_out = low(low_back(jnp.einsum('sgemf,efd->sgemd', activated, down_rows, precision=highest_precision)))
    returned = jnp.einsum('sgtc,sgcd->sgtd', dispatch, expert_out.reshape(SEQS, N_GRP, EXPERTS * MOST, D), precision=highest_precision)
    return residual_stream + gate_prob[..., None] * returned.reshape(SEQS, SEQ_LEN, D)

def reference(tokens, segment_ids, expert_ids, rel_bucket, query_key_value_weight, output_weight, router_weight, gain_attn, gain_ffn, rel_table, w_up, w_down, out_grad):
    weights = tuple((weight_arr.astype(jnp.float32) for weight_arr in (query_key_value_weight, output_weight, router_weight, gain_attn, gain_ffn, rel_table, w_up, w_down)))
    group_total = BATCH // SEQS
    input_tokens = tokens.astype(jnp.float32).reshape(group_total, SEQS, SEQ_LEN, D)
    seg_all = segment_ids.reshape(group_total, SEQS, SEQ_LEN)
    routed = expert_ids.reshape(group_total, SEQS, SEQ_LEN)
    cotangent = out_grad.astype(jnp.float32).reshape(group_total, SEQS, SEQ_LEN, D)

    def one_group(totals, group_data):
        group_in, group_seg, group_routed, group_cot = group_data

        def apply_layer(layer_in, *params):
            return forward(layer_in, group_seg, group_routed, rel_bucket, *params)
        result, pull_back = jax.vjp(apply_layer, group_in, *weights)
        all_grads = pull_back(group_cot)
        totals = jax.tree.map(jnp.add, totals, tuple(all_grads[1:]))
        return (totals, (result.astype(jnp.bfloat16), all_grads[0]))
    zero_grads = tuple((jnp.zeros_like(weight_arr) for weight_arr in weights))
    totals, (outputs, input_grads) = lax.scan(one_group, zero_grads, (input_tokens, seg_all, routed, cotangent))
    layer_out = outputs.reshape(BATCH, SEQ_LEN, D)
    tokens_grad = input_grads.reshape(BATCH, SEQ_LEN, D)
    return (layer_out, tokens_grad, totals[0], totals[1], totals[2], totals[3], totals[4], totals[5], totals[6], totals[7])
```

```python
import functools

import jax
import jax.numpy as jnp
import numpy as np
from jax import lax
from jax.experimental import pallas as pl
from jax.experimental.pallas import tpu as pltpu
from jax.sharding import PartitionSpec as P

eps_norm = 1e-06
neg_fill = -1e30
CORES = 2
PAIR = 2
INSTANCES = 4
F32 = jnp.float32
BF16 = jnp.bfloat16


def rms_parts(values, gain_vec):
    inverse = lax.rsqrt(jnp.mean(values * values, axis=-1, keepdims=True) + eps_norm)
    return (inverse, values * inverse * gain_vec)


def rms_back(grad_normed, values, inverse, gain_vec):
    scaled = grad_normed * gain_vec
    grad_gain = jnp.sum(grad_normed * values * inverse, axis=(0, 1))
    grad_values = inverse * (
        scaled - values * inverse * inverse * jnp.mean(scaled * values, axis=-1, keepdims=True)
    )
    return (grad_values, grad_gain)


def dot_nn(a, b):
    return lax.dot_general(a, b, (((1,), (0,)), ((), ())), preferred_element_type=F32)


def dot_nt(a, b):
    return lax.dot_general(a, b, (((1,), (1,)), ((), ())), preferred_element_type=F32)


def dot_tn(a, b):
    return lax.dot_general(a, b, (((0,), (0,)), ((), ())), preferred_element_type=F32)


def bias_tables(win_ref, table_ref, head, blocks, tile):
    width = win_ref.shape[-1]
    for b in range(blocks):
        row = win_ref[0, head * blocks + b : head * blocks + b + 1, :]
        spread = jnp.broadcast_to(row, (tile, width))
        table_ref[b] = pltpu.roll(spread, width - (tile - 1), 1, stride=1, stride_axis=0)


def bias_tile(table_ref, a, blocks, tile, span):
    start = span - tile - tile * a
    return jnp.concatenate([table_ref[b, :, start : start + span] for b in range(blocks)], axis=1)


def head_lanes(rows, width, head):
    lane = lax.broadcasted_iota(jnp.int32, (rows, width), 1)
    size = width // PAIR
    return (lane >= head * size) & (lane < (head + 1) * size)


def attention_kernel(scale, q_ref, k_ref, v_ref, seg_q_ref, seg_k_ref, win_ref, o_ref, table_ref):
    blocks, tile = table_ref.shape[0], table_ref.shape[1]
    span, width = q_ref.shape[1], q_ref.shape[2]
    keys, values = k_ref[0], v_ref[0]
    seg_keys = seg_k_ref[0]
    for head in range(PAIR):
        bias_tables(win_ref, table_ref, head, blocks, tile)
        mine = head_lanes(tile, width, head)
        for a in range(span // tile):
            rows = slice(a * tile, (a + 1) * tile)
            queries = q_ref[0, rows, :]
            queries = jnp.where(mine, queries * scale, jnp.zeros_like(queries))
            scores = dot_nt(queries, keys) + bias_tile(table_ref, a, blocks, tile, span)
            scores = jnp.where(seg_q_ref[0, rows, :] == seg_keys, scores, neg_fill)
            parts = jnp.exp(scores - jnp.max(scores, axis=1, keepdims=True))
            total = jnp.sum(parts, axis=1, keepdims=True)
            out = (dot_nn(parts.astype(BF16), values) / total).astype(BF16)
            if head == 0:
                o_ref[0, rows, :] = out
            else:
                o_ref[0, rows, :] = jnp.where(mine, out, o_ref[0, rows, :])


def attention_back_kernel(
    scale,
    q_ref,
    k_ref,
    v_ref,
    do_ref,
    seg_q_ref,
    seg_k_ref,
    win_ref,
    dq_ref,
    dk_ref,
    dv_ref,
    diag_ref,
    table_ref,
    sum_ref,
    dk_acc,
    dv_acc,
):
    blocks, tile = table_ref.shape[0], table_ref.shape[1]
    span, width = q_ref.shape[1], q_ref.shape[2]
    keys, values = k_ref[0], v_ref[0]
    seg_keys = seg_k_ref[0]
    dk_acc[...] = jnp.zeros_like(dk_acc)
    dv_acc[...] = jnp.zeros_like(dv_acc)
    for head in range(PAIR):
        bias_tables(win_ref, table_ref, head, blocks, tile)
        sum_ref[...] = jnp.zeros_like(sum_ref)
        mine = head_lanes(tile, width, head)
        for a in range(span // tile):
            rows = slice(a * tile, (a + 1) * tile)
            queries = q_ref[0, rows, :]
            queries = jnp.where(mine, queries * scale, jnp.zeros_like(queries))
            grad_out = do_ref[0, rows, :]
            grad_out = jnp.where(mine, grad_out, jnp.zeros_like(grad_out))
            scores = dot_nt(queries, keys) + bias_tile(table_ref, a, blocks, tile, span)
            scores = jnp.where(seg_q_ref[0, rows, :] == seg_keys, scores, neg_fill)
            parts = jnp.exp(scores - jnp.max(scores, axis=1, keepdims=True))
            probs = parts * (1.0 / jnp.sum(parts, axis=1, keepdims=True))
            grad_probs = dot_nt(grad_out, values)
            delta = jnp.sum(probs * grad_probs, axis=1, keepdims=True)
            grad_scores = (probs * (grad_probs - delta)).astype(BF16)
            dv_acc[...] += dot_tn(grad_out, probs.astype(BF16))
            dk_acc[...] += dot_tn(queries, grad_scores)
            dq = (dot_nn(grad_scores, keys) * scale.astype(np.float32)).astype(BF16)
            if head == 0:
                dq_ref[0, rows, :] = dq
            else:
                dq_ref[0, rows, :] = jnp.where(mine, dq, dq_ref[0, rows, :])
            wide = grad_scores.astype(F32)
            start = span - tile - tile * a
            for b in range(blocks):
                sum_ref[b, :, start : start + span] += wide[:, b * span : (b + 1) * span]
        for b in range(blocks):
            folded = sum_ref[b]
            lanes = folded.shape[1]
            left = tile
            while left > 1:
                left //= 2
                folded = folded[:left] + pltpu.roll(folded[left:], lanes - left, 1)
            at = head * blocks + b
            diag_ref[0, 0, at : at + 1, :] = pltpu.roll(folded, tile - 1, 1)
    dk_ref[0] = dk_acc[...].T.astype(BF16)
    dv_ref[0] = dv_acc[...].T.astype(BF16)


def attention_specs(seqs, span, length, width, pairs, blocks):
    q_spec = pl.BlockSpec((1, span, width), lambda s, h: (s, 0, h))
    k_spec = pl.BlockSpec((1, length, width), lambda s, h: (s, 0, pairs + h))
    v_spec = pl.BlockSpec((1, length, width), lambda s, h: (s, 0, 2 * pairs + h))
    seg_q_spec = pl.BlockSpec((1, span, 1), lambda s, h: (s, 0, 0))
    seg_k_spec = pl.BlockSpec((1, 1, length), lambda s, h: (s, 0, 0))
    win_spec = pl.BlockSpec((1, PAIR * blocks, 2 * span), lambda s, h: (h, 0, 0))
    return q_spec, k_spec, v_spec, seg_q_spec, seg_k_spec, win_spec


def attention(projected, seg_own, seg_all, window, span, head_count):
    seqs, length, total = projected.shape
    model = total // 3
    pairs, width = head_count // PAIR, model // head_count * PAIR
    blocks = length // span
    tile = min(span, 256)
    scale = np.asarray((model // head_count) ** (-0.5), dtype=BF16)
    q_spec, k_spec, v_spec, seg_q_spec, seg_k_spec, win_spec = attention_specs(
        seqs, span, length, width, pairs, blocks
    )
    return pl.pallas_call(
        functools.partial(attention_kernel, scale),
        grid=(seqs, pairs),
        in_specs=[q_spec, k_spec, v_spec, seg_q_spec, seg_k_spec, win_spec],
        out_specs=q_spec,
        out_shape=jax.ShapeDtypeStruct((seqs, span, model), BF16),
        scratch_shapes=[pltpu.VMEM((blocks, tile, 2 * span), F32)],
        compiler_params=pltpu.CompilerParams(vmem_limit_bytes=48 * 1024 * 1024),
        cost_estimate=pl.CostEstimate(
            flops=4 * seqs * span * length * model,
            bytes_accessed=8 * seqs * length * model,
            transcendentals=seqs * head_count * span * length,
        ),
    )(projected, projected, projected, seg_own[:, :, None], seg_all[:, None, :], window)


def attention_back(projected, grad_attended, seg_own, seg_all, window, span, head_count):
    seqs, length, total = projected.shape
    model = total // 3
    pairs, width = head_count // PAIR, model // head_count * PAIR
    blocks = length // span
    tile = min(span, 256)
    scale = np.asarray((model // head_count) ** (-0.5), dtype=BF16)
    q_spec, k_spec, v_spec, seg_q_spec, seg_k_spec, win_spec = attention_specs(
        seqs, span, length, width, pairs, blocks
    )
    key_spec = pl.BlockSpec((1, length, width), lambda s, h: (s, 0, h))
    diag_spec = pl.BlockSpec((1, 1, PAIR * blocks, 2 * span), lambda s, h: (s, h, 0, 0))
    return pl.pallas_call(
        functools.partial(attention_back_kernel, scale),
        grid=(seqs, pairs),
        in_specs=[q_spec, k_spec, v_spec, q_spec, seg_q_spec, seg_k_spec, win_spec],
        out_specs=[q_spec, key_spec, key_spec, diag_spec],
        out_shape=[
            jax.ShapeDtypeStruct((seqs, span, model), BF16),
            jax.ShapeDtypeStruct((seqs, length, model), BF16),
            jax.ShapeDtypeStruct((seqs, length, model), BF16),
            jax.ShapeDtypeStruct((seqs, pairs, PAIR * blocks, 2 * span), F32),
        ],
        scratch_shapes=[
            pltpu.VMEM((blocks, tile, 2 * span), F32),
            pltpu.VMEM((blocks, tile, 2 * span), F32),
            pltpu.VMEM((width, length), F32),
            pltpu.VMEM((width, length), F32),
        ],
        compiler_params=pltpu.CompilerParams(vmem_limit_bytes=48 * 1024 * 1024),
        cost_estimate=pl.CostEstimate(
            flops=10 * seqs * span * length * model,
            bytes_accessed=16 * seqs * length * model,
            transcendentals=seqs * head_count * span * length,
        ),
    )(
        projected,
        projected,
        projected,
        grad_attended,
        seg_own[:, :, None],
        seg_all[:, None, :],
        window,
    )


def expert_kernel(
    core_ref,
    x_ref,
    cot_ref,
    gate_ref,
    up_ref,
    down_ref,
    out_ref,
    grad_in_ref,
    grad_up_ref,
    grad_down_ref,
    grad_out,
    out_acc,
    in_acc,
):
    step = pl.program_id(1)
    rows_in = x_ref[0]

    @pl.when(step == 0)
    def _():
        grad_out[...] = (cot_ref[0].astype(F32) * gate_ref[0]).astype(BF16)
        out_acc[...] = jnp.zeros_like(out_acc)
        in_acc[...] = jnp.zeros_like(in_acc)

    grad_rows = grad_out[...]
    up, down = up_ref[0, 0], down_ref[0, 0]
    pre = dot_nt(rows_in, up)
    grad_act = dot_nt(grad_rows, down)
    slope = np.sqrt(2.0 / np.pi).astype(np.float32)
    square = pre * pre
    tanh = jnp.tanh(slope * (pre + 0.044715 * (square * pre)))
    half = 0.5 * (1.0 + tanh)
    act = (pre * half).astype(BF16)
    inner = slope * (1.0 + (3.0 * 0.044715) * square)
    grad_pre = (grad_act * (half + (0.5 * pre) * (1.0 - tanh * tanh) * inner)).astype(BF16)
    grad_down_ref[0] = dot_tn(act, grad_rows).astype(BF16)
    grad_up_ref[0] = dot_tn(grad_pre, rows_in).astype(BF16)
    out_acc[...] += dot_nn(act, down)
    in_acc[...] += dot_nn(grad_pre, up)

    @pl.when(step == pl.num_programs(1) - 1)
    def _():
        out_ref[0] = out_acc[...].astype(BF16)
        grad_in_ref[0] = in_acc[...].astype(BF16)


def run_experts(core, rows_in, cot, gate, up, down, first, count):
    _, slots, model = rows_in.shape
    part = up.shape[2]
    tile = next(t for t in (512, 384, 256, 128, part) if part % t == 0 and slots * t <= 1 << 18 or t == part)
    row_spec = pl.BlockSpec((1, slots, model), lambda e, f, c: (first + e, 0, 0))
    gate_spec = pl.BlockSpec((1, slots, 1), lambda e, f, c: (first + e, 0, 0))
    weight_spec = pl.BlockSpec((1, 1, tile, model), lambda e, f, c: (first + e, c[0], f, 0))
    out_spec = pl.BlockSpec((1, slots, model), lambda e, f, c: (e, 0, 0))
    grad_spec = pl.BlockSpec((1, tile, model), lambda e, f, c: (e, f, 0))
    return pl.pallas_call(
        expert_kernel,
        grid_spec=pltpu.PrefetchScalarGridSpec(
            num_scalar_prefetch=1,
            grid=(count, part // tile),
            in_specs=[row_spec, row_spec, gate_spec, weight_spec, weight_spec],
            out_specs=[out_spec, out_spec, grad_spec, grad_spec],
            scratch_shapes=[
                pltpu.VMEM((slots, model), BF16),
                pltpu.VMEM((slots, model), F32),
                pltpu.VMEM((slots, model), F32),
            ],
        ),
        out_shape=[
            jax.ShapeDtypeStruct((count, slots, model), BF16),
            jax.ShapeDtypeStruct((count, slots, model), BF16),
            jax.ShapeDtypeStruct((count, part, model), BF16),
            jax.ShapeDtypeStruct((count, part, model), BF16),
        ],
        compiler_params=pltpu.CompilerParams(vmem_limit_bytes=56 * 1024 * 1024),
        cost_estimate=pl.CostEstimate(
            flops=12 * count * slots * part * model,
            bytes_accessed=8 * count * part * model,
            transcendentals=count * slots * part,
        ),
    )(core, rows_in, cot, gate, up, down)


def ring_order(chips):
    return list(range(0, chips, 2)) + list(range(chips - 1 - chips % 2, 0, -2))


def ring_sum(parts, place, order):
    chips = len(order)
    hop = [
        (order[i] * CORES + c, order[(i + 1) % chips] * CORES + c)
        for i in range(chips)
        for c in range(CORES)
    ]

    def pick(index):
        return lax.dynamic_index_in_dim(parts, index % chips, 0, keepdims=False)

    held = pick(place)
    for step in range(chips - 1):
        arrived = lax.ppermute(held, "rep", hop)
        held = (arrived.astype(F32) + pick(place - step - 1 + chips).astype(F32)).astype(BF16)
    found = [((place + 1) % chips, held)]
    for step in range(chips - 1):
        held = lax.ppermute(held, "rep", hop)
        found.append(((place - step + chips) % chips, held))
    return found


def swap_cores(values, reps):
    return lax.ppermute(values, "rep", [(r, r ^ 1) for r in range(reps)])


def swap_groups(values):
    return lax.ppermute(values, "grp", [(0, 1), (1, 0)])


def local(
    tokens,
    segment_ids,
    expert_ids,
    rel_bucket,
    query_key_value_weight,
    output_weight,
    router_weight,
    gain_attn,
    gain_ffn,
    rel_table,
    w_up,
    w_down,
    out_grad,
):
    groups = lax.axis_size("grp")
    reps = lax.axis_size("rep")
    chips = reps // CORES
    grp_index = lax.axis_index("grp")
    rep_index = lax.axis_index("rep")
    core, chip = rep_index % CORES, rep_index // CORES
    seqs, span, model = tokens.shape
    length = span * groups
    head_count = rel_table.shape[1]
    buckets = rel_table.shape[0] * groups
    experts = router_weight.shape[1]
    owned = experts // groups
    most = span // 4
    slots = most * seqs
    hidden = w_up.shape[0] // owned
    part = hidden // CORES
    two = groups == 2

    def gather_rotated(values, axis):
        if two:
            return jnp.concatenate([values, swap_groups(values)], axis=axis)
        whole = lax.all_gather(values, "grp", axis=axis, tiled=True)
        return jnp.roll(whole, -grp_index * values.shape[axis], axis=axis)

    def gather_stacked(values):
        if two:
            other = swap_groups(values)
            return jnp.where(
                grp_index == 0, jnp.stack([values, other]), jnp.stack([other, values])
            )
        return lax.all_gather(values, "grp", axis=0)

    def gather_weight(values):
        if not two:
            return lax.all_gather(values, "grp", axis=0, tiled=True)
        rows = values.shape[0]
        piece = rows // CORES
        mine = swap_groups(lax.dynamic_slice_in_dim(values, core * piece, piece, 0))
        theirs = swap_cores(mine, reps)
        whole = jnp.zeros((2 * rows,) + values.shape[1:], values.dtype)
        whole = lax.dynamic_update_slice_in_dim(whole, values, grp_index * rows, 0)
        start = (1 - grp_index) * rows
        whole = lax.dynamic_update_slice_in_dim(whole, mine, start + core * piece, 0)
        return lax.dynamic_update_slice_in_dim(whole, theirs, start + (1 - core) * piece, 0)

    small = jnp.concatenate(
        [router_weight.reshape(-1), gain_attn, gain_ffn, rel_table.reshape(-1)]
    )
    small = gather_stacked(small)
    cuts = np.cumsum([router_weight.size, gain_attn.size, gain_ffn.size]).tolist()
    full_router, full_gain_attn, full_gain_ffn, full_table = jnp.split(small, cuts, axis=1)
    full_router = full_router.reshape(model, experts)
    full_table = full_table.reshape(buckets, head_count)
    gain_one = full_gain_attn.reshape(-1).astype(F32)
    gain_two = full_gain_ffn.reshape(-1).astype(F32)
    full_qkv = gather_weight(query_key_value_weight)
    tokens_all = gather_rotated(tokens, 1)
    seg_all = gather_rotated(segment_ids, 1)
    full_out = gather_weight(output_weight)

    first_expert = grp_index * owned if two else 0
    expert_of = expert_ids[..., 0]
    chosen = expert_of[..., None] == jnp.arange(experts)
    chosen_float = chosen.astype(F32)
    strict_lower = (jnp.arange(span)[:, None] > jnp.arange(span)[None, :]).astype(BF16)
    earlier = jnp.einsum("tu,sue->ste", strict_lower, chosen.astype(BF16), preferred_element_type=F32)
    slot_rank = jnp.sum(earlier * chosen_float, axis=-1).astype(jnp.int32)
    slot_index = (expert_of - first_expert + experts) % experts * most + slot_rank
    in_slot = slot_index[..., None] == jnp.arange(experts * most)
    dispatch = in_slot.astype(BF16)

    def to_slots(rows):
        placed = jnp.einsum("stc,std->csd", dispatch, rows, preferred_element_type=F32)
        return placed.astype(BF16).reshape(experts, slots, model)

    def to_side(placed):
        if two:
            return jnp.concatenate([placed[:owned], swap_groups(placed[owned:])], axis=1)
        moved = lax.all_to_all(
            placed.reshape((groups, owned) + placed.shape[1:]), "grp", 0, 0, tiled=False
        )
        return jnp.moveaxis(moved, 0, 1).reshape((owned, groups * slots) + placed.shape[2:])

    def from_side(rows):
        if two:
            return jnp.concatenate([rows[:, :slots], swap_groups(rows[:, slots:])], axis=0)
        moved = jnp.moveaxis(rows.reshape(owned, groups, slots, model), 1, 0)
        return lax.all_to_all(moved, "grp", 0, 0, tiled=False).reshape(experts, slots, model)

    def to_cores(rows):
        return jnp.concatenate([rows, swap_cores(rows, reps)], axis=1)

    cot_rows = to_cores(to_side(to_slots(out_grad)))

    input_tokens = tokens.astype(F32)
    inverse_one, normed_own = rms_parts(input_tokens, gain_one)
    normed_own = normed_own.astype(BF16)
    normed_all = rms_parts(tokens_all.astype(F32), gain_one)[1].astype(BF16)
    projected = jnp.einsum(
        "std,de->ste", normed_all, full_qkv, preferred_element_type=F32
    ).astype(BF16)

    bucket_hot = (rel_bucket[None, :] == jnp.arange(buckets)[:, None]).astype(BF16)
    bucket_hot = jnp.pad(bucket_hot, ((0, 0), (0, 1)))
    bias_line = jnp.einsum("bh,bo->ho", full_table, bucket_hot, preferred_element_type=F32)
    starts = [
        ((grp_index + b) % groups - grp_index) * span + length - span for b in range(groups)
    ]
    window = jnp.stack(
        [lax.dynamic_slice_in_dim(bias_line, at, 2 * span, 1) for at in starts], axis=1
    ).reshape(head_count // PAIR, PAIR * groups, 2 * span)

    attended = attention(projected, segment_ids, seg_all, window, span, head_count)
    residual = input_tokens + jnp.einsum(
        "std,de->ste", attended, full_out, preferred_element_type=F32
    )
    inverse_two, normed_ffn = rms_parts(residual, gain_two)
    normed_ffn = normed_ffn.astype(BF16)
    router_logits = jnp.einsum(
        "std,de->ste", normed_ffn, full_router, preferred_element_type=F32
    )
    router = jax.nn.softmax(router_logits, axis=-1)
    gate_prob = jnp.sum(router * chosen_float, axis=-1)
    gate_slots = jnp.sum(jnp.where(in_slot, gate_prob[..., None], 0.0), axis=1)
    gate_slots = jnp.moveaxis(gate_slots.reshape(seqs, experts, most), 0, 2).reshape(experts, slots)

    expert_in = to_cores(to_side(to_slots(normed_ffn)))
    gate_rows = to_cores(to_side(gate_slots))[..., None]
    up_parts = w_up.reshape(owned, CORES, part, model)
    down_parts = w_down.reshape(owned, CORES, part, model)
    core_id = core.astype(jnp.int32).reshape(1)
    batches = min(INSTANCES, owned)
    count = owned // batches
    outs, grad_ins, grad_ups, grad_downs = [], [], [], []
    for i in range(batches):
        results = run_experts(
            core_id, expert_in, cot_rows, gate_rows, up_parts, down_parts, i * count, count
        )
        for kept, result in zip((outs, grad_ins, grad_ups, grad_downs), results):
            kept.append(result)

    def finish(partials):
        rows = jnp.concatenate(partials, axis=0)
        near = rows.shape[1] // CORES
        both = rows[:, :near].astype(F32) + swap_cores(rows[:, near:], reps).astype(F32)
        placed = from_side(both.astype(BF16))
        return jnp.einsum(
            "stc,csd->std",
            dispatch,
            placed.reshape(experts * most, seqs, model),
            preferred_element_type=F32,
        )

    order = ring_order(chips)
    shard = part // chips
    gathered = []
    for grads, way in ((grad_ups, order), (grad_downs, order[::-1])):
        place = jnp.asarray(np.argsort(way), jnp.int32)[chip]
        whole = jnp.zeros((owned, CORES, chips, shard, model), F32)
        for i, grad in enumerate(grads):
            parts = jnp.moveaxis(grad.reshape(count, chips, shard, model), 1, 0)
            for index, piece in ring_sum(parts.reshape(chips, count * shard, model), place, way):
                other = swap_cores(piece, reps)
                for at, value in ((core, piece), (1 - core, other)):
                    value = value.astype(F32).reshape(count, 1, 1, shard, model)
                    whole = lax.dynamic_update_slice(whole, value, (i * count, at, index, 0, 0))
        gathered.append(whole.reshape(owned * hidden, model))

    returned = finish(outs)
    layer_out = (residual + gate_prob[..., None] * returned).astype(BF16)
    cotangent = out_grad.astype(F32)
    grad_gate = jnp.sum(cotangent * returned, axis=-1)
    grad_from_experts = finish(grad_ins)
    grad_logits = (grad_gate[..., None] * router * (chosen_float - gate_prob[..., None])).astype(
        BF16
    )
    grad_router = jnp.einsum("std,ste->de", normed_ffn, grad_logits, preferred_element_type=F32)
    grad_normed_ffn = grad_from_experts + jnp.einsum(
        "ste,de->std", grad_logits, full_router, preferred_element_type=F32
    )
    grad_mid, grad_gain_ffn = rms_back(grad_normed_ffn, residual, inverse_two, gain_two)
    grad_residual = cotangent + grad_mid
    grad_attn = grad_residual.astype(BF16)
    grad_wout = jnp.einsum("std,ste->de", attended, grad_attn, preferred_element_type=F32)
    grad_attended = jnp.einsum(
        "ste,de->std", grad_attn, full_out, preferred_element_type=F32
    ).astype(BF16)
    grad_queries, key_terms, value_terms, diagonals = attention_back(
        projected, grad_attended, segment_ids, seg_all, window, span, head_count
    )
    diagonals = jnp.sum(diagonals, axis=0).reshape(head_count, groups, 2 * span)
    hot_window = jnp.stack(
        [lax.dynamic_slice_in_dim(bucket_hot, at, 2 * span, 1) for at in starts], axis=1
    ).astype(F32)
    grad_table = jnp.einsum("bno,hno->bh", hot_window, diagonals, precision=lax.Precision.HIGHEST)

    def own_keys(terms):
        if two:
            return terms[:, :span].astype(F32) + swap_groups(terms[:, span:]).astype(F32)
        terms = jnp.roll(terms, grp_index * span, axis=1)
        return lax.psum_scatter(terms, "grp", scatter_dimension=1, tiled=True)

    grad_keys, grad_values = own_keys(key_terms), own_keys(value_terms)
    grad_mixed = jnp.concatenate(
        [grad_queries, grad_keys.astype(BF16), grad_values.astype(BF16)], axis=-1
    )
    grad_qkv = jnp.einsum("std,ste->de", normed_own, grad_mixed, preferred_element_type=F32)
    grad_normed = jnp.einsum("ste,de->std", grad_mixed, full_qkv, preferred_element_type=F32)
    grad_input_part, grad_gain_attn = rms_back(grad_normed, input_tokens, inverse_one, gain_one)
    tokens_grad = grad_residual + grad_input_part

    shares = tuple(
        lax.psum_scatter(value.astype(BF16), "grp", scatter_dimension=0, tiled=True)
        for value in (grad_qkv, grad_wout, grad_router, grad_gain_attn, grad_gain_ffn, grad_table)
    )
    sums = tuple(value.astype(F32) for value in lax.psum(shares, "rep"))
    return (layer_out, tokens_grad) + sums + tuple(gathered)


def solution(mesh):
    return jax.shard_map(
        local,
        mesh=mesh,
        in_specs=(
            P("rep", "grp", None),
            P("rep", "grp"),
            P("rep", "grp", None),
            P(),
            P("grp", None),
            P("grp", None),
            P("grp", None),
            P("grp"),
            P("grp"),
            P("grp", None),
            P("grp", None),
            P("grp", None),
            P("rep", "grp", None),
        ),
        out_specs=(
            P("rep", "grp", None),
            P("rep", "grp", None),
            P("grp", None),
            P("grp", None),
            P("grp", None),
            P("grp"),
            P("grp"),
            P("grp", None),
            P("grp", None),
            P("grp", None),
        ),
        check_vma=False,
    )
```

```python
import functools

import jax
import jax.numpy as jnp
import numpy as np
from jax import lax
from jax.experimental import pallas as pl
from jax.experimental.pallas import tpu as pltpu
from jax.sharding import PartitionSpec as P

eps_norm = 1e-06
neg_fill = -1e30
CORES = 2
PAIR = 2
F32 = jnp.float32
BF16 = jnp.bfloat16


def rms_parts(values, gain_vec):
    inverse = lax.rsqrt(jnp.mean(values * values, axis=-1, keepdims=True) + eps_norm)
    return (inverse, values * inverse * gain_vec)


def rms_back(grad_normed, values, inverse, gain_vec):
    scaled = grad_normed * gain_vec
    grad_gain = jnp.sum(grad_normed * values * inverse, axis=(0, 1))
    grad_values = inverse * (
        scaled - values * inverse * inverse * jnp.mean(scaled * values, axis=-1, keepdims=True)
    )
    return (grad_values, grad_gain)


def dot_nn(a, b):
    return lax.dot_general(a, b, (((1,), (0,)), ((), ())), preferred_element_type=F32)


def dot_nt(a, b):
    return lax.dot_general(a, b, (((1,), (1,)), ((), ())), preferred_element_type=F32)


def dot_tn(a, b):
    return lax.dot_general(a, b, (((0,), (0,)), ((), ())), preferred_element_type=F32)


def bias_tables(win_ref, table_ref, head, blocks, tile):
    width = win_ref.shape[-1]
    for b in range(blocks):
        row = win_ref[0, head * blocks + b : head * blocks + b + 1, :]
        spread = jnp.broadcast_to(row, (tile, width))
        table_ref[b] = pltpu.roll(spread, width - (tile - 1), 1, stride=1, stride_axis=0)


def bias_tile(table_ref, a, blocks, tile, span):
    start = span - tile - tile * a
    return jnp.concatenate([table_ref[b, :, start : start + span] for b in range(blocks)], axis=1)


def head_lanes(rows, width, head):
    lane = lax.broadcasted_iota(jnp.int32, (rows, width), 1)
    size = width // PAIR
    return (lane >= head * size) & (lane < (head + 1) * size)


def attention_kernel(scale, q_ref, k_ref, v_ref, seg_q_ref, seg_k_ref, win_ref, o_ref, table_ref):
    blocks, tile = table_ref.shape[0], table_ref.shape[1]
    span, width = q_ref.shape[1], q_ref.shape[2]
    keys, values = k_ref[0], v_ref[0]
    seg_keys = seg_k_ref[0]
    for head in range(PAIR):
        bias_tables(win_ref, table_ref, head, blocks, tile)
        mine = head_lanes(tile, width, head)
        for a in range(span // tile):
            rows = slice(a * tile, (a + 1) * tile)
            queries = q_ref[0, rows, :]
            queries = jnp.where(mine, queries * scale, jnp.zeros_like(queries))
            scores = dot_nt(queries, keys) + bias_tile(table_ref, a, blocks, tile, span)
            scores = jnp.where(seg_q_ref[0, rows, :] == seg_keys, scores, neg_fill)
            parts = jnp.exp(scores - jnp.max(scores, axis=1, keepdims=True))
            total = jnp.sum(parts, axis=1, keepdims=True)
            out = (dot_nn(parts.astype(BF16), values) / total).astype(BF16)
            if head == 0:
                o_ref[0, rows, :] = out
            else:
                o_ref[0, rows, :] = jnp.where(mine, out, o_ref[0, rows, :])


def attention_back_kernel(
    scale,
    q_ref,
    k_ref,
    v_ref,
    do_ref,
    seg_q_ref,
    seg_k_ref,
    win_ref,
    dq_ref,
    dk_ref,
    dv_ref,
    diag_ref,
    table_ref,
    sum_ref,
    dk_acc,
    dv_acc,
):
    blocks, tile = table_ref.shape[0], table_ref.shape[1]
    span, width = q_ref.shape[1], q_ref.shape[2]
    keys, values = k_ref[0], v_ref[0]
    seg_keys = seg_k_ref[0]
    dk_acc[...] = jnp.zeros_like(dk_acc)
    dv_acc[...] = jnp.zeros_like(dv_acc)
    for head in range(PAIR):
        bias_tables(win_ref, table_ref, head, blocks, tile)
        sum_ref[...] = jnp.zeros_like(sum_ref)
        mine = head_lanes(tile, width, head)
        for a in range(span // tile):
            rows = slice(a * tile, (a + 1) * tile)
            queries = q_ref[0, rows, :]
            queries = jnp.where(mine, queries * scale, jnp.zeros_like(queries))
            grad_out = do_ref[0, rows, :]
            grad_out = jnp.where(mine, grad_out, jnp.zeros_like(grad_out))
            scores = dot_nt(queries, keys) + bias_tile(table_ref, a, blocks, tile, span)
            scores = jnp.where(seg_q_ref[0, rows, :] == seg_keys, scores, neg_fill)
            parts = jnp.exp(scores - jnp.max(scores, axis=1, keepdims=True))
            probs = parts * (1.0 / jnp.sum(parts, axis=1, keepdims=True))
            grad_probs = dot_nt(grad_out, values)
            delta = jnp.sum(probs * grad_probs, axis=1, keepdims=True)
            grad_scores = (probs * (grad_probs - delta)).astype(BF16)
            dv_acc[...] += dot_tn(grad_out, probs.astype(BF16))
            dk_acc[...] += dot_tn(queries, grad_scores)
            dq = (dot_nn(grad_scores, keys) * scale.astype(np.float32)).astype(BF16)
            if head == 0:
                dq_ref[0, rows, :] = dq
            else:
                dq_ref[0, rows, :] = jnp.where(mine, dq, dq_ref[0, rows, :])
            wide = grad_scores.astype(F32)
            start = span - tile - tile * a
            for b in range(blocks):
                sum_ref[b, :, start : start + span] += wide[:, b * span : (b + 1) * span]
        for b in range(blocks):
            folded = sum_ref[b]
            lanes = folded.shape[1]
            left = tile
            while left > 1:
                left //= 2
                folded = folded[:left] + pltpu.roll(folded[left:], lanes - left, 1)
            at = head * blocks + b
            diag_ref[0, 0, at : at + 1, :] = pltpu.roll(folded, tile - 1, 1)
    dk_ref[0] = dk_acc[...].T.astype(BF16)
    dv_ref[0] = dv_acc[...].T.astype(BF16)


def attention_specs(seqs, span, length, width, pairs, blocks):
    q_spec = pl.BlockSpec((1, span, width), lambda s, h: (s, 0, h))
    k_spec = pl.BlockSpec((1, length, width), lambda s, h: (s, 0, pairs + h))
    v_spec = pl.BlockSpec((1, length, width), lambda s, h: (s, 0, 2 * pairs + h))
    seg_q_spec = pl.BlockSpec((1, span, 1), lambda s, h: (s, 0, 0))
    seg_k_spec = pl.BlockSpec((1, 1, length), lambda s, h: (s, 0, 0))
    win_spec = pl.BlockSpec((1, PAIR * blocks, 2 * span), lambda s, h: (h, 0, 0))
    return q_spec, k_spec, v_spec, seg_q_spec, seg_k_spec, win_spec


def attention(projected, seg_own, seg_all, window, span, head_count):
    seqs, length, total = projected.shape
    model = total // 3
    pairs, width = head_count // PAIR, model // head_count * PAIR
    blocks = length // span
    tile = min(span, 256)
    scale = np.asarray((model // head_count) ** (-0.5), dtype=BF16)
    q_spec, k_spec, v_spec, seg_q_spec, seg_k_spec, win_spec = attention_specs(
        seqs, span, length, width, pairs, blocks
    )
    return pl.pallas_call(
        functools.partial(attention_kernel, scale),
        grid=(seqs, pairs),
        in_specs=[q_spec, k_spec, v_spec, seg_q_spec, seg_k_spec, win_spec],
        out_specs=q_spec,
        out_shape=jax.ShapeDtypeStruct((seqs, span, model), BF16),
        scratch_shapes=[pltpu.VMEM((blocks, tile, 2 * span), F32)],
        compiler_params=pltpu.CompilerParams(vmem_limit_bytes=48 * 1024 * 1024),
        cost_estimate=pl.CostEstimate(
            flops=4 * seqs * span * length * model,
            bytes_accessed=8 * seqs * length * model,
            transcendentals=seqs * head_count * span * length,
        ),
    )(projected, projected, projected, seg_own[:, :, None], seg_all[:, None, :], window)


def attention_back(projected, grad_attended, seg_own, seg_all, window, span, head_count):
    seqs, length, total = projected.shape
    model = total // 3
    pairs, width = head_count // PAIR, model // head_count * PAIR
    blocks = length // span
    tile = min(span, 256)
    scale = np.asarray((model // head_count) ** (-0.5), dtype=BF16)
    q_spec, k_spec, v_spec, seg_q_spec, seg_k_spec, win_spec = attention_specs(
        seqs, span, length, width, pairs, blocks
    )
    key_spec = pl.BlockSpec((1, length, width), lambda s, h: (s, 0, h))
    diag_spec = pl.BlockSpec((1, 1, PAIR * blocks, 2 * span), lambda s, h: (s, h, 0, 0))
    return pl.pallas_call(
        functools.partial(attention_back_kernel, scale),
        grid=(seqs, pairs),
        in_specs=[q_spec, k_spec, v_spec, q_spec, seg_q_spec, seg_k_spec, win_spec],
        out_specs=[q_spec, key_spec, key_spec, diag_spec],
        out_shape=[
            jax.ShapeDtypeStruct((seqs, span, model), BF16),
            jax.ShapeDtypeStruct((seqs, length, model), BF16),
            jax.ShapeDtypeStruct((seqs, length, model), BF16),
            jax.ShapeDtypeStruct((seqs, pairs, PAIR * blocks, 2 * span), F32),
        ],
        scratch_shapes=[
            pltpu.VMEM((blocks, tile, 2 * span), F32),
            pltpu.VMEM((blocks, tile, 2 * span), F32),
            pltpu.VMEM((width, length), F32),
            pltpu.VMEM((width, length), F32),
        ],
        compiler_params=pltpu.CompilerParams(vmem_limit_bytes=48 * 1024 * 1024),
        cost_estimate=pl.CostEstimate(
            flops=10 * seqs * span * length * model,
            bytes_accessed=16 * seqs * length * model,
            transcendentals=seqs * head_count * span * length,
        ),
    )(
        projected,
        projected,
        projected,
        grad_attended,
        seg_own[:, :, None],
        seg_all[:, None, :],
        window,
    )


def expert_kernel(
    pieces,
    core_ref,
    *refs,
):
    x_refs, cot_refs, gate_refs = (refs[i * pieces : (i + 1) * pieces] for i in range(3))
    up_ref, down_ref, out_ref, grad_in_ref, grad_up_ref, grad_down_ref = refs[3 * pieces : -4]
    rows_all, grad_out, out_acc, in_acc = refs[-4:]
    step = pl.program_id(1)

    @pl.when(step == 0)
    def _():
        start = 0
        for x_ref, cot_ref, gate_ref in zip(x_refs, cot_refs, gate_refs):
            rows = slice(start, start + x_ref.shape[1])
            start = rows.stop
            rows_all[rows, :] = x_ref[0]
            gate = jnp.broadcast_to(gate_ref[0], (128, x_ref.shape[1])).T[:, :1]
            grad_out[rows, :] = (cot_ref[0].astype(F32) * gate).astype(BF16)
        out_acc[...] = jnp.zeros_like(out_acc)
        in_acc[...] = jnp.zeros_like(in_acc)

    rows_in = rows_all[...]
    grad_rows = grad_out[...]
    up, down = up_ref[0, 0], down_ref[0, 0]
    pre = dot_nt(rows_in, up)
    grad_act = dot_nt(grad_rows, down)
    slope = np.sqrt(2.0 / np.pi).astype(np.float32)
    square = pre * pre
    tanh = jnp.tanh(slope * (pre + 0.044715 * (square * pre)))
    half = 0.5 * (1.0 + tanh)
    act = (pre * half).astype(BF16)
    inner = slope * (1.0 + (3.0 * 0.044715) * square)
    grad_pre = (grad_act * (half + (0.5 * pre) * (1.0 - tanh * tanh) * inner)).astype(BF16)
    grad_down_ref[0] = dot_tn(act, grad_rows).astype(BF16)
    grad_up_ref[0] = dot_tn(grad_pre, rows_in).astype(BF16)
    out_acc[...] += dot_nn(act, down)
    in_acc[...] += dot_nn(grad_pre, up)

    @pl.when(step == pl.num_programs(1) - 1)
    def _():
        out_ref[0] = out_acc[...].astype(BF16)
        grad_in_ref[0] = in_acc[...].astype(BF16)


def run_experts(core, rows_in, cot, gate, up, down, first, count):
    model = rows_in[0].shape[2]
    sizes = [piece.shape[1] for piece in rows_in]
    slots = sum(sizes)
    part = up.shape[2]
    fits = [t for t in (512, 384, 256, 128) if part % t == 0 and slots * t <= 1 << 18]
    tile = (fits + [part])[0]
    row_specs = [pl.BlockSpec((1, n, model), lambda e, f, c: (first + e, 0, 0)) for n in sizes]
    gate_specs = [pl.BlockSpec((1, 1, n), lambda e, f, c: (first + e, 0, 0)) for n in sizes]
    weight_spec = pl.BlockSpec((1, 1, tile, model), lambda e, f, c: (first + e, c[0], f, 0))
    out_spec = pl.BlockSpec((1, slots, model), lambda e, f, c: (e, 0, 0))
    grad_spec = pl.BlockSpec((1, tile, model), lambda e, f, c: (e, f, 0))
    return pl.pallas_call(
        functools.partial(expert_kernel, len(sizes)),
        grid_spec=pltpu.PrefetchScalarGridSpec(
            num_scalar_prefetch=1,
            grid=(count, part // tile),
            in_specs=row_specs + row_specs + gate_specs + [weight_spec, weight_spec],
            out_specs=[out_spec, out_spec, grad_spec, grad_spec],
            scratch_shapes=[
                pltpu.VMEM((slots, model), BF16),
                pltpu.VMEM((slots, model), BF16),
                pltpu.VMEM((slots, model), F32),
                pltpu.VMEM((slots, model), F32),
            ],
        ),
        out_shape=[
            jax.ShapeDtypeStruct((count, slots, model), BF16),
            jax.ShapeDtypeStruct((count, slots, model), BF16),
            jax.ShapeDtypeStruct((count, part, model), BF16),
            jax.ShapeDtypeStruct((count, part, model), BF16),
        ],
        compiler_params=pltpu.CompilerParams(vmem_limit_bytes=56 * 1024 * 1024),
        cost_estimate=pl.CostEstimate(
            flops=12 * count * slots * part * model,
            bytes_accessed=8 * count * part * model,
            transcendentals=count * slots * part,
        ),
    )(core, *rows_in, *cot, *gate, up, down)


class Ring:
    def __init__(self, parts, chip, forward):
        self.parts = parts
        self.chips = chips = parts.shape[1]
        order = list(range(0, chips, 2)) + list(range(chips - 1 - chips % 2, 0, -2))
        self.place = jnp.where(chip % 2 == 0, chip // 2, chips - 1 - chip // 2)
        if not forward:
            order, self.place = order[::-1], chips - 1 - self.place
        self.hop = [
            (order[i] * CORES + c, order[(i + 1) % chips] * CORES + c)
            for i in range(chips)
            for c in range(CORES)
        ]
        self.held = self.pick(0)

    def index(self, ahead):
        return (self.place + ahead + self.chips) % self.chips

    def pick(self, ahead):
        return lax.dynamic_slice_in_dim(self.parts, self.index(ahead), 1, 1)

    def move(self):
        return lax.ppermute(self.held, "rep", self.hop)

    def take(self, step, arrived):
        if step < self.chips - 1:
            arrived = (arrived.astype(F32) + self.pick(-step - 1).astype(F32)).astype(BF16)
        self.held = arrived


def tie(rings, values):
    held, values = lax.optimization_barrier(([ring.held for ring in rings], values))
    for ring, kept in zip(rings, held):
        ring.held = kept
    return values


def fresh(shape, amount):
    return pl.pallas_call(
        lambda *refs: None,
        out_shape=[jax.ShapeDtypeStruct(shape, F32) for _ in range(amount)],
        out_specs=[pl.BlockSpec(memory_space=pl.ANY) for _ in range(amount)],
    )()


def swap_reps(values, reps, bit):
    return lax.ppermute(values, "rep", [(r, r ^ bit) for r in range(reps)])


def swap_cores(values, reps):
    return swap_reps(values, reps, 1)


def swap_groups(values):
    return lax.ppermute(values, "grp", [(0, 1), (1, 0)])


def local(
    tokens,
    segment_ids,
    expert_ids,
    rel_bucket,
    query_key_value_weight,
    output_weight,
    router_weight,
    gain_attn,
    gain_ffn,
    rel_table,
    w_up,
    w_down,
    out_grad,
):
    groups = lax.axis_size("grp")
    reps = lax.axis_size("rep")
    chips = reps // CORES
    grp_index = lax.axis_index("grp")
    rep_index = lax.axis_index("rep")
    core, chip = rep_index % CORES, rep_index // CORES
    seqs, span, model = tokens.shape
    length = span * groups
    head_count = rel_table.shape[1]
    buckets = rel_table.shape[0] * groups
    experts = router_weight.shape[1]
    owned = experts // groups
    most = span // 4
    slots = most * seqs
    hidden = w_up.shape[0] // owned
    part = hidden // CORES
    two = groups == 2

    def gather_rotated(values, axis):
        if two:
            return jnp.concatenate([values, swap_groups(values)], axis=axis)
        whole = lax.all_gather(values, "grp", axis=axis, tiled=True)
        return jnp.roll(whole, -grp_index * values.shape[axis], axis=axis)

    def gather_stacked(values):
        if two:
            other = swap_groups(values)
            return jnp.where(
                grp_index == 0, jnp.stack([values, other]), jnp.stack([other, values])
            )
        return lax.all_gather(values, "grp", axis=0)

    def gather_weight(values, after=None):
        if not two:
            return lax.all_gather(values, "grp", axis=0, tiled=True)
        rows = values.shape[0]
        sharers = 4 if reps % 4 == 0 and rows % 64 == 0 else 2
        piece = rows // sharers
        place = rep_index % sharers
        pieces = {0: swap_groups(lax.dynamic_slice_in_dim(values, place * piece, piece, 0))}
        if sharers == 4:
            pieces[2] = swap_reps(pieces[0], reps, 2)
            if after is not None:
                pieces[2], after[0] = lax.optimization_barrier((pieces[2], after[0]))
        for bit in list(pieces):
            pieces[bit | 1] = swap_cores(pieces[bit], reps)
        whole = jnp.zeros((2 * rows,) + values.shape[1:], values.dtype)
        whole = lax.dynamic_update_slice_in_dim(whole, values, grp_index * rows, 0)
        start = (1 - grp_index) * rows
        for bit, fetched in pieces.items():
            whole = lax.dynamic_update_slice_in_dim(
                whole, fetched, start + (place ^ bit) * piece, 0
            )
        return whole

    small = jnp.concatenate(
        [router_weight.reshape(-1), gain_attn, gain_ffn, rel_table.reshape(-1)]
    )
    small = gather_stacked(small)
    cuts = np.cumsum([router_weight.size, gain_attn.size, gain_ffn.size]).tolist()
    full_router, full_gain_attn, full_gain_ffn, full_table = jnp.split(small, cuts, axis=1)
    full_router = full_router.reshape(model, experts)
    full_table = full_table.reshape(buckets, head_count)
    gain_one = full_gain_attn.reshape(-1).astype(F32)
    gain_two = full_gain_ffn.reshape(-1).astype(F32)
    seg_all = gather_rotated(segment_ids, 1)
    arriving = [gather_rotated(tokens, 1)]
    full_qkv = gather_weight(query_key_value_weight, arriving)
    tokens_all = arriving[0]

    first_expert = grp_index * owned if two else 0
    expert_of = expert_ids[..., 0]
    chosen = expert_of[..., None] == jnp.arange(experts)
    chosen_float = chosen.astype(F32)
    strict_lower = (jnp.arange(span)[:, None] > jnp.arange(span)[None, :]).astype(BF16)
    earlier = jnp.einsum("tu,sue->ste", strict_lower, chosen.astype(BF16), preferred_element_type=F32)
    slot_rank = jnp.sum(earlier * chosen_float, axis=-1).astype(jnp.int32)
    slot_index = (expert_of - first_expert + experts) % experts * most + slot_rank
    in_slot = slot_index[..., None] == jnp.arange(experts * most)
    dispatch = in_slot.astype(BF16)

    def to_slots(rows):
        placed = jnp.einsum("stc,std->csd", dispatch, rows, preferred_element_type=F32)
        return placed.astype(BF16).reshape(experts, slots, model)

    def to_side(*arrays):
        if two:
            far = lax.optimization_barrier([swap_groups(placed[owned:]) for placed in arrays])
            near = [[placed[:owned], other] for placed, other in zip(arrays, far)]
        else:
            near = []
            for placed in arrays:
                split = placed.reshape((groups, owned) + placed.shape[1:])
                moved = lax.all_to_all(split, "grp", 0, 0, tiled=False)
                near.append([moved[i] for i in range(groups)])
        both = [pieces + [swap_cores(piece, reps) for piece in pieces] for pieces in near]
        return both if len(both) > 1 else both[0]

    def from_side(rows):
        if two:
            return jnp.concatenate([rows[:, :slots], swap_groups(rows[:, slots:])], axis=0)
        moved = jnp.moveaxis(rows.reshape(owned, groups, slots, model), 1, 0)
        return lax.all_to_all(moved, "grp", 0, 0, tiled=False).reshape(experts, slots, model)

    input_tokens = tokens.astype(F32)
    inverse_one, normed_own = rms_parts(input_tokens, gain_one)
    normed_own = normed_own.astype(BF16)
    normed_all = rms_parts(tokens_all.astype(F32), gain_one)[1].astype(BF16)
    projected = jnp.einsum(
        "std,de->ste", normed_all, full_qkv, preferred_element_type=F32
    ).astype(BF16)

    bucket_line = jnp.pad(rel_bucket, (0, 1), constant_values=buckets)
    starts = [
        ((grp_index + b) % groups - grp_index) * span + length - span for b in range(groups)
    ]
    bucket_window = jnp.stack(
        [lax.dynamic_slice_in_dim(bucket_line, at, 2 * span, 0) for at in starts]
    )
    bucket_hot = bucket_window[None] == jnp.arange(buckets)[:, None, None]
    bucket_hot = bucket_hot.reshape(buckets, groups * 2 * span)
    window = jnp.einsum(
        "bh,bo->ho", full_table, bucket_hot.astype(BF16), preferred_element_type=F32
    ).reshape(head_count // PAIR, PAIR * groups, 2 * span)

    cot_slots = to_slots(out_grad)
    projected, late_out, cot_slots = lax.optimization_barrier(
        (projected, output_weight, cot_slots)
    )
    full_out = gather_weight(late_out)
    cot_rows = to_side(cot_slots)

    attended = attention(projected, segment_ids, seg_all, window, span, head_count)
    residual = input_tokens + jnp.einsum(
        "std,de->ste", attended, full_out, preferred_element_type=F32
    )
    inverse_two, normed_ffn = rms_parts(residual, gain_two)
    normed_ffn = normed_ffn.astype(BF16)
    router_logits = jnp.einsum(
        "std,de->ste", normed_ffn, full_router, preferred_element_type=F32
    )
    router = jax.nn.softmax(router_logits, axis=-1)
    gate_prob = jnp.sum(router * chosen_float, axis=-1)
    gate_slots = jnp.sum(jnp.where(in_slot, gate_prob[..., None], 0.0), axis=1)
    gate_slots = jnp.moveaxis(gate_slots.reshape(seqs, experts, most), 0, 2).reshape(experts, slots)

    expert_in, gate_rows = to_side(to_slots(normed_ffn), gate_slots[:, None, :])
    up_parts = w_up.reshape(owned, CORES, part, model)
    down_parts = w_down.reshape(owned, CORES, part, model)
    shard = part // chips

    sets, outs, grad_ins = [], [], []
    amounts = [owned]
    for i, count in enumerate(amounts):
        first = sum(amounts[:i])
        out, grad_in, grad_up, grad_down = run_experts(
            core.astype(jnp.int32).reshape(1),
            expert_in,
            cot_rows,
            gate_rows,
            up_parts,
            down_parts,
            first,
            count,
        )
        outs.append(out)
        grad_ins.append(grad_in)
        rings = [
            Ring(grad.reshape(count, chips, shard, model), chip, forward)
            for grad, forward in ((grad_up, True), (grad_down, False))
        ]
        if i + 1 < len(amounts):
            expert_in = tie(rings, expert_in)
        sets.append((first, rings))
    total_rounds = 2 * (chips - 1)
    rounds = iter(range(total_rounds))

    def swap_held(held):
        return [[swap_cores(piece, reps) for piece in pieces] for pieces in held]

    def store(wholes, held, others, ahead):
        stored = list(wholes)
        for (first, rings), pieces, swapped in zip(sets, held, others):
            for i, (ring, piece, other) in enumerate(zip(rings, pieces, swapped)):
                for at, value in ((core, piece), (1 - core, other)):
                    stored[i] = lax.dynamic_update_slice(
                        stored[i],
                        value.astype(F32)[:, None],
                        (first, at, ring.index(ahead), 0, 0),
                    )
        return stored

    wholes = []

    def beside(stage=None, ins=()):
        step = next(rounds, None)
        if step is None:
            return stage(*ins) if stage else ()
        ins, kept = tie(sets[-1][1], (ins, list(wholes)))
        held = [[ring.held for ring in rings] for _, rings in sets]
        arrived = [[ring.move() for ring in rings] for _, rings in sets]
        if step == chips - 2:
            kept = list(fresh((owned, CORES, chips, shard, model), 2))
        if step >= chips - 1:
            others, ins = lax.optimization_barrier((swap_held(held), ins))
            kept = store(kept, held, others, chips - step)
        results = stage(*ins) if stage else ()
        arrived[0], results, kept = lax.optimization_barrier((arrived[0], results, kept))
        for (_, rings), values in zip(sets, arrived):
            for ring, value in zip(rings, values):
                ring.take(step, value)
        wholes[:] = kept
        return results

    def side_sums(outs, grad_ins):
        sums = []
        for rows in (outs, grad_ins):
            rows = jnp.concatenate(rows, axis=0)
            near = rows.shape[1] // CORES
            both = rows[:, :near].astype(F32) + swap_cores(rows[:, near:], reps).astype(F32)
            sums.append(both.astype(BF16))
        return from_side(sums[0]), sums[1]

    def to_tokens(placed):
        return jnp.einsum(
            "stc,csd->std",
            dispatch,
            placed.reshape(experts * most, seqs, model),
            preferred_element_type=F32,
        )

    cotangent = out_grad.astype(F32)

    def ffn_end(placed, grad_sums):
        grad_placed = from_side(grad_sums)
        returned = to_tokens(placed)
        layer_out = (residual + gate_prob[..., None] * returned).astype(BF16)
        grad_gate = jnp.sum(cotangent * returned, axis=-1)
        grad_logits = grad_gate[..., None] * router * (chosen_float - gate_prob[..., None])
        grad_logits = grad_logits.astype(BF16)
        grad_router = jnp.einsum("std,ste->de", normed_ffn, grad_logits, preferred_element_type=F32)
        grad_normed_ffn = to_tokens(grad_placed) + jnp.einsum(
            "ste,de->std", grad_logits, full_router, preferred_element_type=F32
        )
        grad_mid, grad_gain_ffn = rms_back(grad_normed_ffn, residual, inverse_two, gain_two)
        grad_residual = cotangent + grad_mid
        grad_attn = grad_residual.astype(BF16)
        grad_attended = jnp.einsum(
            "ste,de->std", grad_attn, full_out, preferred_element_type=F32
        ).astype(BF16)
        return layer_out, grad_router, grad_gain_ffn, grad_residual, grad_attn, grad_attended

    def scores_back(grad_attended):
        return attention_back(
            projected, grad_attended, segment_ids, seg_all, window, span, head_count
        )

    def own_keys(terms):
        if two:
            total = terms[:, :span].astype(F32) + swap_groups(terms[:, span:]).astype(F32)
            return total.astype(BF16)
        terms = jnp.roll(terms, grp_index * span, axis=1)
        return lax.psum_scatter(terms, "grp", scatter_dimension=1, tiled=True)

    def keys_end(key_terms, diagonals, grad_attn):
        grad_wout = jnp.einsum("std,ste->de", attended, grad_attn, preferred_element_type=F32)
        diagonals = jnp.sum(diagonals, axis=0).reshape(head_count, groups * 2 * span)
        grad_table = jnp.einsum(
            "bo,ho->bh", bucket_hot.astype(F32), diagonals, precision=lax.Precision.HIGHEST
        )
        return own_keys(key_terms), grad_table, grad_wout

    def projection_back(grad_queries, grad_keys, value_terms, grad_residual):
        grad_values = own_keys(value_terms)
        grad_mixed = jnp.concatenate([grad_queries, grad_keys, grad_values], axis=-1)
        grad_qkv = jnp.einsum("std,ste->de", normed_own, grad_mixed, preferred_element_type=F32)
        grad_normed = jnp.einsum("ste,de->std", grad_mixed, full_qkv, preferred_element_type=F32)
        grad_input_part, grad_gain_attn = rms_back(
            grad_normed, input_tokens, inverse_one, gain_one
        )
        return grad_qkv.astype(BF16), grad_gain_attn, grad_residual + grad_input_part

    placed, grad_sums = beside(side_sums, (outs, grad_ins))
    layer_out, grad_router, grad_gain_ffn, grad_residual, grad_attn, grad_attended = beside(
        ffn_end, (placed, grad_sums)
    )
    grad_queries, key_terms, value_terms, diagonals = beside(scores_back, (grad_attended,))
    grad_keys, grad_table, grad_wout = beside(keys_end, (key_terms, diagonals, grad_attn))
    grad_qkv, grad_gain_attn, tokens_grad = beside(
        projection_back, (grad_queries, grad_keys, value_terms, grad_residual)
    )

    tiny = (grad_router, grad_gain_attn, grad_gain_ffn, grad_table)
    tiny = [value.astype(BF16).reshape(groups, -1) for value in tiny]
    tiny_cuts = np.cumsum([value.shape[1] for value in tiny]).tolist()
    flat = jnp.concatenate(tiny, axis=1)
    flat = jnp.pad(flat, ((0, 0), (0, -flat.shape[1] % model))).reshape(groups, -1, model)
    rows_out = model // groups
    rows_qkv = 3 * rows_out
    rows_all = rows_qkv + rows_out + flat.shape[1]
    packed = jnp.concatenate(
        [
            grad_qkv.astype(BF16).reshape(groups, -1, model),
            grad_wout.astype(BF16).reshape(groups, -1, model),
            jnp.pad(flat, ((0, 0), (0, -rows_all % (reps * 8)), (0, 0))),
        ],
        axis=1,
    )
    packed = packed.reshape(groups, CORES, -1, model)

    def halve(values, axis, place, swap):
        mine = lax.dynamic_index_in_dim(values, place, axis, keepdims=False)
        given = swap(lax.dynamic_index_in_dim(values, 1 - place, axis, keepdims=False))
        return (mine.astype(F32) + given.astype(F32)).astype(BF16)

    def share(packed):
        values = halve(packed, 1, core, lambda v: swap_cores(v, reps))
        if two:
            return halve(values, 0, grp_index, swap_groups)
        return lax.psum_scatter(values, "grp", scatter_dimension=0, tiled=False)

    parts = beside(share, (packed,)).reshape(chips, -1, model)

    upward, downward = chips // 2, chips - 1 - chips // 2
    place, up_hop, down_hop = rings[0].place, rings[0].hop, rings[1].hop

    def pick(ahead):
        index = (place + ahead + chips) % chips
        return lax.dynamic_index_in_dim(parts, index, 0, keepdims=False).astype(F32)

    def put(whole, value, ahead):
        index = (place + ahead + chips) % chips
        return lax.dynamic_update_slice_in_dim(whole, value[None], index, 0)

    def reduce_stage(step):
        def stage(above, below):
            above = lax.ppermute(above, "rep", up_hop)
            if step < upward - 1:
                above = (above.astype(F32) + pick(upward - 1 - step)).astype(BF16)
            if step < downward:
                below = lax.ppermute(below, "rep", down_hop)
            if step < downward - 1:
                below = (below.astype(F32) + pick(step + 1 - downward)).astype(BF16)
            return above, below

        return stage

    def gather_stage(step):
        def stage(above, below, whole):
            above = lax.ppermute(above, "rep", up_hop)
            whole = put(whole, above, -1 - step)
            if step < downward:
                below = lax.ppermute(below, "rep", down_hop)
                whole = put(whole, below, 1 + step)
            return above, below, whole

        return stage

    above, below = pick(upward).astype(BF16), pick(-downward).astype(BF16)
    for step in range(upward):
        above, below = beside(reduce_stage(step), (above, below))
    own_sum = (above.astype(F32) + below.astype(F32) + pick(0)).astype(BF16)
    above = below = own_sum
    whole = put(jnp.zeros_like(parts), own_sum, 0)
    for step in range(upward):
        above, below, whole = beside(gather_stage(step), (above, below, whole))
    whole = whole.reshape(1, -1, model)
    others = swap_cores(whole, reps)
    sums = jnp.where(
        core == 0,
        jnp.concatenate([whole, others], axis=0),
        jnp.concatenate([others, whole], axis=0),
    )
    for _ in range(total_rounds - 6 - 2 * upward):
        beside()

    def unpack(sums):
        sums = sums.reshape(-1, model)
        tiny = jnp.split(
            sums[rows_qkv + rows_out : rows_all].astype(F32).reshape(-1), tiny_cuts
        )
        return (
            sums[:rows_qkv].astype(F32).reshape(model // groups, 3 * model),
            sums[rows_qkv : rows_qkv + rows_out].astype(F32),
            tiny[0].reshape(model // groups, experts),
            tiny[1],
            tiny[2],
            tiny[3].reshape(buckets // groups, head_count),
        )

    small_sums = unpack(sums)
    held = [[ring.held for ring in rings] for _, rings in sets]
    wholes = store(wholes, held, swap_held(held), 2 - chips)
    gathered = tuple(whole.reshape(owned * hidden, model) for whole in wholes)
    return (layer_out, tokens_grad) + small_sums + gathered


def solution(mesh):
    return jax.shard_map(
        local,
        mesh=mesh,
        in_specs=(
            P("rep", "grp", None),
            P("rep", "grp"),
            P("rep", "grp", None),
            P(),
            P("grp", None),
            P("grp", None),
            P("grp", None),
            P("grp"),
            P("grp"),
            P("grp", None),
            P("grp", None),
            P("grp", None),
            P("rep", "grp", None),
        ),
        out_specs=(
            P("rep", "grp", None),
            P("rep", "grp", None),
            P("grp", None),
            P("grp", None),
            P("grp", None),
            P("grp"),
            P("grp"),
            P("grp", None),
            P("grp", None),
            P("grp", None),
        ),
        check_vma=False,
    )
```

```python
import functools

import jax
import jax.numpy as jnp
import numpy as np
from jax import lax
from jax.experimental import pallas as pl
from jax.experimental.pallas import tpu as pltpu
from jax.sharding import PartitionSpec as P

eps_norm = 1e-06
neg_fill = -1e30
CORES = 2
PAIR = 2
F32 = jnp.float32
BF16 = jnp.bfloat16


def rms_parts(values, gain_vec):
    inverse = lax.rsqrt(jnp.mean(values * values, axis=-1, keepdims=True) + eps_norm)
    return (inverse, values * inverse * gain_vec)


def rms_back(grad_normed, values, inverse, gain_vec):
    scaled = grad_normed * gain_vec
    grad_gain = jnp.sum(grad_normed * values * inverse, axis=(0, 1))
    grad_values = inverse * (
        scaled - values * inverse * inverse * jnp.mean(scaled * values, axis=-1, keepdims=True)
    )
    return (grad_values, grad_gain)


def dot_nn(a, b):
    return lax.dot_general(a, b, (((1,), (0,)), ((), ())), preferred_element_type=F32)


def dot_nt(a, b):
    return lax.dot_general(a, b, (((1,), (1,)), ((), ())), preferred_element_type=F32)


def dot_tn(a, b):
    return lax.dot_general(a, b, (((0,), (0,)), ((), ())), preferred_element_type=F32)


def bias_tables(win_ref, table_ref, head, blocks, tile):
    width = win_ref.shape[-1]
    for b in range(blocks):
        row = win_ref[0, head * blocks + b : head * blocks + b + 1, :]
        spread = jnp.broadcast_to(row, (tile, width))
        table_ref[b] = pltpu.roll(spread, width - (tile - 1), 1, stride=1, stride_axis=0)


def bias_tile(table_ref, a, blocks, tile, span):
    start = span - tile - tile * a
    return jnp.concatenate([table_ref[b, :, start : start + span] for b in range(blocks)], axis=1)


def head_lanes(rows, width, head):
    lane = lax.broadcasted_iota(jnp.int32, (rows, width), 1)
    size = width // PAIR
    return (lane >= head * size) & (lane < (head + 1) * size)


def attention_kernel(scale, q_ref, k_ref, v_ref, seg_q_ref, seg_k_ref, win_ref, o_ref, table_ref):
    blocks, tile = table_ref.shape[0], table_ref.shape[1]
    span, width = q_ref.shape[1], q_ref.shape[2]
    keys, values = k_ref[0], v_ref[0]
    seg_keys = seg_k_ref[0]
    for head in range(PAIR):
        bias_tables(win_ref, table_ref, head, blocks, tile)
        mine = head_lanes(tile, width, head)
        for a in range(span // tile):
            rows = slice(a * tile, (a + 1) * tile)
            queries = q_ref[0, rows, :]
            queries = jnp.where(mine, queries * scale, jnp.zeros_like(queries))
            scores = dot_nt(queries, keys) + bias_tile(table_ref, a, blocks, tile, span)
            scores = jnp.where(seg_q_ref[0, rows, :] == seg_keys, scores, neg_fill)
            parts = jnp.exp(scores - jnp.max(scores, axis=1, keepdims=True))
            total = jnp.sum(parts, axis=1, keepdims=True)
            out = (dot_nn(parts.astype(BF16), values) / total).astype(BF16)
            if head == 0:
                o_ref[0, rows, :] = out
            else:
                o_ref[0, rows, :] = jnp.where(mine, out, o_ref[0, rows, :])


def attention_back_kernel(
    scale,
    q_ref,
    k_ref,
    v_ref,
    do_ref,
    seg_q_ref,
    seg_k_ref,
    win_ref,
    dq_ref,
    dk_ref,
    dv_ref,
    diag_ref,
    table_ref,
    sum_ref,
    dk_acc,
    dv_acc,
):
    blocks, tile = table_ref.shape[0], table_ref.shape[1]
    span, width = q_ref.shape[1], q_ref.shape[2]
    keys, values = k_ref[0], v_ref[0]
    seg_keys = seg_k_ref[0]
    dk_acc[...] = jnp.zeros_like(dk_acc)
    dv_acc[...] = jnp.zeros_like(dv_acc)
    for head in range(PAIR):
        bias_tables(win_ref, table_ref, head, blocks, tile)
        sum_ref[...] = jnp.zeros_like(sum_ref)
        mine = head_lanes(tile, width, head)
        for a in range(span // tile):
            rows = slice(a * tile, (a + 1) * tile)
            queries = q_ref[0, rows, :]
            queries = jnp.where(mine, queries * scale, jnp.zeros_like(queries))
            grad_out = do_ref[0, rows, :]
            grad_out = jnp.where(mine, grad_out, jnp.zeros_like(grad_out))
            scores = dot_nt(queries, keys) + bias_tile(table_ref, a, blocks, tile, span)
            scores = jnp.where(seg_q_ref[0, rows, :] == seg_keys, scores, neg_fill)
            parts = jnp.exp(scores - jnp.max(scores, axis=1, keepdims=True))
            probs = parts * (1.0 / jnp.sum(parts, axis=1, keepdims=True))
            grad_probs = dot_nt(grad_out, values)
            delta = jnp.sum(probs * grad_probs, axis=1, keepdims=True)
            grad_scores = (probs * (grad_probs - delta)).astype(BF16)
            dv_acc[...] += dot_tn(grad_out, probs.astype(BF16))
            dk_acc[...] += dot_tn(queries, grad_scores)
            dq = (dot_nn(grad_scores, keys) * scale.astype(np.float32)).astype(BF16)
            if head == 0:
                dq_ref[0, rows, :] = dq
            else:
                dq_ref[0, rows, :] = jnp.where(mine, dq, dq_ref[0, rows, :])
            wide = grad_scores.astype(F32)
            start = span - tile - tile * a
            for b in range(blocks):
                sum_ref[b, :, start : start + span] += wide[:, b * span : (b + 1) * span]
        for b in range(blocks):
            folded = sum_ref[b]
            lanes = folded.shape[1]
            left = tile
            while left > 1:
                left //= 2
                folded = folded[:left] + pltpu.roll(folded[left:], lanes - left, 1)
            at = head * blocks + b
            diag_ref[0, 0, at : at + 1, :] = pltpu.roll(folded, tile - 1, 1)
    dk_ref[0] = dk_acc[...].T.astype(BF16)
    dv_ref[0] = dv_acc[...].T.astype(BF16)


def attention_specs(seqs, span, length, width, pairs, blocks):
    q_spec = pl.BlockSpec((1, span, width), lambda s, h: (s, 0, h))
    k_spec = pl.BlockSpec((1, length, width), lambda s, h: (s, 0, pairs + h))
    v_spec = pl.BlockSpec((1, length, width), lambda s, h: (s, 0, 2 * pairs + h))
    seg_q_spec = pl.BlockSpec((1, span, 1), lambda s, h: (s, 0, 0))
    seg_k_spec = pl.BlockSpec((1, 1, length), lambda s, h: (s, 0, 0))
    win_spec = pl.BlockSpec((1, PAIR * blocks, 2 * span), lambda s, h: (h, 0, 0))
    return q_spec, k_spec, v_spec, seg_q_spec, seg_k_spec, win_spec


def attention(projected, seg_own, seg_all, window, span, head_count):
    seqs, length, total = projected.shape
    model = total // 3
    pairs, width = head_count // PAIR, model // head_count * PAIR
    blocks = length // span
    tile = min(span, 256)
    scale = np.asarray((model // head_count) ** (-0.5), dtype=BF16)
    q_spec, k_spec, v_spec, seg_q_spec, seg_k_spec, win_spec = attention_specs(
        seqs, span, length, width, pairs, blocks
    )
    return pl.pallas_call(
        functools.partial(attention_kernel, scale),
        grid=(seqs, pairs),
        in_specs=[q_spec, k_spec, v_spec, seg_q_spec, seg_k_spec, win_spec],
        out_specs=q_spec,
        out_shape=jax.ShapeDtypeStruct((seqs, span, model), BF16),
        scratch_shapes=[pltpu.VMEM((blocks, tile, 2 * span), F32)],
        compiler_params=pltpu.CompilerParams(vmem_limit_bytes=48 * 1024 * 1024),
        cost_estimate=pl.CostEstimate(
            flops=4 * seqs * span * length * model,
            bytes_accessed=8 * seqs * length * model,
            transcendentals=seqs * head_count * span * length,
        ),
    )(projected, projected, projected, seg_own[:, :, None], seg_all[:, None, :], window)


def attention_back(projected, grad_attended, seg_own, seg_all, window, span, head_count):
    seqs, length, total = projected.shape
    model = total // 3
    pairs, width = head_count // PAIR, model // head_count * PAIR
    blocks = length // span
    tile = min(span, 256)
    scale = np.asarray((model // head_count) ** (-0.5), dtype=BF16)
    q_spec, k_spec, v_spec, seg_q_spec, seg_k_spec, win_spec = attention_specs(
        seqs, span, length, width, pairs, blocks
    )
    key_spec = pl.BlockSpec((1, length, width), lambda s, h: (s, 0, h))
    diag_spec = pl.BlockSpec((1, 1, PAIR * blocks, 2 * span), lambda s, h: (s, h, 0, 0))
    return pl.pallas_call(
        functools.partial(attention_back_kernel, scale),
        grid=(seqs, pairs),
        in_specs=[q_spec, k_spec, v_spec, q_spec, seg_q_spec, seg_k_spec, win_spec],
        out_specs=[q_spec, key_spec, key_spec, diag_spec],
        out_shape=[
            jax.ShapeDtypeStruct((seqs, span, model), BF16),
            jax.ShapeDtypeStruct((seqs, length, model), BF16),
            jax.ShapeDtypeStruct((seqs, length, model), BF16),
            jax.ShapeDtypeStruct((seqs, pairs, PAIR * blocks, 2 * span), F32),
        ],
        scratch_shapes=[
            pltpu.VMEM((blocks, tile, 2 * span), F32),
            pltpu.VMEM((blocks, tile, 2 * span), F32),
            pltpu.VMEM((width, length), F32),
            pltpu.VMEM((width, length), F32),
        ],
        compiler_params=pltpu.CompilerParams(vmem_limit_bytes=48 * 1024 * 1024),
        cost_estimate=pl.CostEstimate(
            flops=10 * seqs * span * length * model,
            bytes_accessed=16 * seqs * length * model,
            transcendentals=seqs * head_count * span * length,
        ),
    )(
        projected,
        projected,
        projected,
        grad_attended,
        seg_own[:, :, None],
        seg_all[:, None, :],
        window,
    )


def expert_kernel(
    pieces,
    core_ref,
    *refs,
):
    x_refs, cot_refs, gate_refs = (refs[i * pieces : (i + 1) * pieces] for i in range(3))
    up_ref, down_ref, out_ref, grad_in_ref, grad_up_ref, grad_down_ref = refs[3 * pieces : -4]
    rows_all, grad_out, out_acc, in_acc = refs[-4:]
    step = pl.program_id(1)

    @pl.when(step == 0)
    def _():
        start = 0
        for x_ref, cot_ref, gate_ref in zip(x_refs, cot_refs, gate_refs):
            rows = slice(start, start + x_ref.shape[1])
            start = rows.stop
            rows_all[rows, :] = x_ref[0]
            gate = jnp.broadcast_to(gate_ref[0], (128, x_ref.shape[1])).T[:, :1]
            grad_out[rows, :] = (cot_ref[0].astype(F32) * gate).astype(BF16)
        out_acc[...] = jnp.zeros_like(out_acc)
        in_acc[...] = jnp.zeros_like(in_acc)

    rows_in = rows_all[...]
    grad_rows = grad_out[...]
    up, down = up_ref[0, 0], down_ref[0, 0]
    pre = dot_nt(rows_in, up)
    grad_act = dot_nt(grad_rows, down)
    slope = np.sqrt(2.0 / np.pi).astype(np.float32)
    square = pre * pre
    tanh = jnp.tanh(slope * (pre + 0.044715 * (square * pre)))
    half = 0.5 * (1.0 + tanh)
    act = (pre * half).astype(BF16)
    inner = slope * (1.0 + (3.0 * 0.044715) * square)
    grad_pre = (grad_act * (half + (0.5 * pre) * (1.0 - tanh * tanh) * inner)).astype(BF16)
    grad_down_ref[0] = dot_tn(act, grad_rows).astype(BF16)
    grad_up_ref[0] = dot_tn(grad_pre, rows_in).astype(BF16)
    out_acc[...] += dot_nn(act, down)
    in_acc[...] += dot_nn(grad_pre, up)

    @pl.when(step == pl.num_programs(1) - 1)
    def _():
        out_ref[0] = out_acc[...].astype(BF16)
        grad_in_ref[0] = in_acc[...].astype(BF16)


def run_experts(core, rows_in, cot, gate, up, down, first, count):
    model = rows_in[0].shape[2]
    sizes = [piece.shape[1] for piece in rows_in]
    slots = sum(sizes)
    part = up.shape[2]
    fits = [t for t in (768, 512, 384, 256, 128) if part % t == 0 and slots * t <= 3 << 17]
    tile = (fits + [part])[0]
    row_specs = [pl.BlockSpec((1, n, model), lambda e, f, c: (first + e, 0, 0)) for n in sizes]
    gate_specs = [pl.BlockSpec((1, 1, n), lambda e, f, c: (first + e, 0, 0)) for n in sizes]
    weight_spec = pl.BlockSpec((1, 1, tile, model), lambda e, f, c: (first + e, c[0], f, 0))
    out_spec = pl.BlockSpec((1, slots, model), lambda e, f, c: (e, 0, 0))
    grad_spec = pl.BlockSpec((1, tile, model), lambda e, f, c: (e, f, 0))
    return pl.pallas_call(
        functools.partial(expert_kernel, len(sizes)),
        grid_spec=pltpu.PrefetchScalarGridSpec(
            num_scalar_prefetch=1,
            grid=(count, part // tile),
            in_specs=row_specs + row_specs + gate_specs + [weight_spec, weight_spec],
            out_specs=[out_spec, out_spec, grad_spec, grad_spec],
            scratch_shapes=[
                pltpu.VMEM((slots, model), BF16),
                pltpu.VMEM((slots, model), BF16),
                pltpu.VMEM((slots, model), F32),
                pltpu.VMEM((slots, model), F32),
            ],
        ),
        out_shape=[
            jax.ShapeDtypeStruct((count, slots, model), BF16),
            jax.ShapeDtypeStruct((count, slots, model), BF16),
            jax.ShapeDtypeStruct((count, part, model), BF16),
            jax.ShapeDtypeStruct((count, part, model), BF16),
        ],
        compiler_params=pltpu.CompilerParams(vmem_limit_bytes=56 * 1024 * 1024),
        cost_estimate=pl.CostEstimate(
            flops=12 * count * slots * part * model,
            bytes_accessed=8 * count * part * model,
            transcendentals=count * slots * part,
        ),
    )(core, *rows_in, *cot, *gate, up, down)


class Ring:
    def __init__(self, parts, chip, forward):
        self.parts = parts
        self.chips = chips = parts.shape[1]
        order = list(range(0, chips, 2)) + list(range(chips - 1 - chips % 2, 0, -2))
        self.place = jnp.where(chip % 2 == 0, chip // 2, chips - 1 - chip // 2)
        if not forward:
            order, self.place = order[::-1], chips - 1 - self.place
        self.hop = [
            (order[i] * CORES + c, order[(i + 1) % chips] * CORES + c)
            for i in range(chips)
            for c in range(CORES)
        ]
        self.held = self.pick(0)

    def index(self, ahead):
        return (self.place + ahead + self.chips) % self.chips

    def pick(self, ahead):
        return lax.dynamic_slice_in_dim(self.parts, self.index(ahead), 1, 1)

    def move(self):
        return lax.ppermute(self.held, "rep", self.hop)


    def take(self, step, arrived):
        if step < self.chips - 1:
            arrived = (arrived.astype(F32) + self.pick(-step - 1).astype(F32)).astype(BF16)
        self.held = arrived


def tie(rings, values):
    held, values = lax.optimization_barrier(([ring.held for ring in rings], values))
    for ring, kept in zip(rings, held):
        ring.held = kept
    return values


def fresh(shape, amount):
    return pl.pallas_call(
        lambda *refs: None,
        out_shape=[jax.ShapeDtypeStruct(shape, F32) for _ in range(amount)],
        out_specs=[pl.BlockSpec(memory_space=pl.ANY) for _ in range(amount)],
    )()


def swap_reps(values, reps, bit):
    return lax.ppermute(values, "rep", [(r, r ^ bit) for r in range(reps)])


def swap_cores(values, reps):
    return swap_reps(values, reps, 1)


def swap_groups(values):
    return lax.ppermute(values, "grp", [(0, 1), (1, 0)])


def local(
    tokens,
    segment_ids,
    expert_ids,
    rel_bucket,
    query_key_value_weight,
    output_weight,
    router_weight,
    gain_attn,
    gain_ffn,
    rel_table,
    w_up,
    w_down,
    out_grad,
):
    groups = lax.axis_size("grp")
    reps = lax.axis_size("rep")
    chips = reps // CORES
    grp_index = lax.axis_index("grp")
    rep_index = lax.axis_index("rep")
    core, chip = rep_index % CORES, rep_index // CORES
    seqs, span, model = tokens.shape
    length = span * groups
    head_count = rel_table.shape[1]
    buckets = rel_table.shape[0] * groups
    experts = router_weight.shape[1]
    owned = experts // groups
    most = span // 4
    slots = most * seqs
    hidden = w_up.shape[0] // owned
    part = hidden // CORES
    two = groups == 2

    def fetch(values):
        return swap_groups(values) if two else lax.all_gather(values, "grp", axis=0)

    def rotated(values, fetched, axis):
        if two:
            return jnp.concatenate([values, fetched], axis=axis)
        whole = jnp.concatenate([fetched[i] for i in range(groups)], axis=axis)
        return jnp.roll(whole, -grp_index * values.shape[axis], axis=axis)

    def stacked(values, fetched):
        if not two:
            return fetched
        return jnp.where(
            grp_index == 0, jnp.stack([values, fetched]), jnp.stack([fetched, values])
        )

    def gather_weight(values, after):
        if not two:
            return lax.all_gather(values, "grp", axis=0, tiled=True), after
        rows = values.shape[0]
        sharers = 4 if reps % 4 == 0 and rows % 64 == 0 else 2
        piece = rows // sharers
        place = rep_index % sharers
        pieces = {0: swap_groups(lax.dynamic_slice_in_dim(values, place * piece, piece, 0))}
        if sharers == 4:
            pieces[2] = swap_reps(pieces[0], reps, 2)
            pieces[2], after = lax.optimization_barrier((pieces[2], after))
        for bit in list(pieces):
            pieces[bit | 1] = swap_cores(pieces[bit], reps)
        whole = jnp.zeros((2 * rows,) + values.shape[1:], values.dtype)
        whole = lax.dynamic_update_slice_in_dim(whole, values, grp_index * rows, 0)
        start = (1 - grp_index) * rows
        for bit, fetched in pieces.items():
            whole = lax.dynamic_update_slice_in_dim(
                whole, fetched, start + (place ^ bit) * piece, 0
            )
        return whole, after

    def gather_whole(values):
        if not two:
            return lax.all_gather(values, "grp", axis=0, tiled=True)
        rows = values.shape[0]
        whole = jnp.zeros((2 * rows,) + values.shape[1:], values.dtype)
        whole = lax.dynamic_update_slice_in_dim(whole, values, grp_index * rows, 0)
        return lax.dynamic_update_slice_in_dim(
            whole, swap_groups(values), (1 - grp_index) * rows, 0
        )

    small = jnp.concatenate(
        [router_weight.reshape(-1), gain_attn, gain_ffn, rel_table.reshape(-1)]
    )
    small_far, tokens_far = fetch(small), fetch(tokens)
    full_qkv, (small_far, tokens_far) = gather_weight(
        query_key_value_weight, (small_far, tokens_far)
    )
    small = stacked(small, small_far)
    cuts = np.cumsum([router_weight.size, gain_attn.size, gain_ffn.size]).tolist()
    full_router, full_gain_attn, full_gain_ffn, full_table = jnp.split(small, cuts, axis=1)
    full_router = full_router.reshape(model, experts)
    full_table = full_table.reshape(buckets, head_count)
    gain_one = full_gain_attn.reshape(-1).astype(F32)
    gain_two = full_gain_ffn.reshape(-1).astype(F32)
    tokens_far, late_out, late_ids = lax.optimization_barrier(
        (tokens_far, output_weight, segment_ids)
    )
    tokens_all = rotated(tokens, tokens_far, 1)
    seg_all = rotated(late_ids, fetch(late_ids), 1)
    full_out = gather_whole(late_out)

    first_expert = grp_index * owned if two else 0
    expert_of = expert_ids[..., 0]
    chosen = expert_of[..., None] == jnp.arange(experts)
    chosen_float = chosen.astype(F32)
    strict_lower = (jnp.arange(span)[:, None] > jnp.arange(span)[None, :]).astype(BF16)
    earlier = jnp.einsum("tu,sue->ste", strict_lower, chosen.astype(BF16), preferred_element_type=F32)
    slot_rank = jnp.sum(earlier * chosen_float, axis=-1).astype(jnp.int32)
    slot_index = (expert_of - first_expert + experts) % experts * most + slot_rank
    in_slot = slot_index[..., None] == jnp.arange(experts * most)
    dispatch = in_slot.astype(BF16)

    def to_slots(rows):
        placed = jnp.einsum("stc,std->csd", dispatch, rows, preferred_element_type=F32)
        return placed.astype(BF16).reshape(experts, slots, model)

    def to_side(*arrays):
        if two:
            far = lax.optimization_barrier([swap_groups(placed[owned:]) for placed in arrays])
            near = [[placed[:owned], other] for placed, other in zip(arrays, far)]
        else:
            near = []
            for placed in arrays:
                split = placed.reshape((groups, owned) + placed.shape[1:])
                moved = lax.all_to_all(split, "grp", 0, 0, tiled=False)
                near.append([moved[i] for i in range(groups)])
        both = [pieces + [swap_cores(piece, reps) for piece in pieces] for pieces in near]
        return both if len(both) > 1 else both[0]

    def from_side(rows):
        if two:
            return jnp.concatenate([rows[:, :slots], swap_groups(rows[:, slots:])], axis=0)
        moved = jnp.moveaxis(rows.reshape(owned, groups, slots, model), 1, 0)
        return lax.all_to_all(moved, "grp", 0, 0, tiled=False).reshape(experts, slots, model)

    input_tokens = tokens.astype(F32)
    inverse_one, normed_own = rms_parts(input_tokens, gain_one)
    normed_own = normed_own.astype(BF16)
    normed_all = rms_parts(tokens_all.astype(F32), gain_one)[1].astype(BF16)
    projected = jnp.einsum(
        "std,de->ste", normed_all, full_qkv, preferred_element_type=F32
    ).astype(BF16)

    projected, cot_slots = lax.optimization_barrier((projected, to_slots(out_grad)))
    cot_rows = to_side(cot_slots)

    bucket_line = jnp.pad(rel_bucket, (0, 1), constant_values=buckets)
    starts = [
        ((grp_index + b) % groups - grp_index) * span + length - span for b in range(groups)
    ]
    bucket_window = jnp.stack(
        [lax.dynamic_slice_in_dim(bucket_line, at, 2 * span, 0) for at in starts]
    )
    bucket_hot = bucket_window[None] == jnp.arange(buckets)[:, None, None]
    bucket_hot = bucket_hot.reshape(buckets, groups * 2 * span)
    window = jnp.einsum(
        "bh,bo->ho", full_table, bucket_hot.astype(BF16), preferred_element_type=F32
    ).reshape(head_count // PAIR, PAIR * groups, 2 * span)

    attended = attention(projected, segment_ids, seg_all, window, span, head_count)
    residual = input_tokens + jnp.einsum(
        "std,de->ste", attended, full_out, preferred_element_type=F32
    )
    inverse_two, normed_ffn = rms_parts(residual, gain_two)
    normed_ffn = normed_ffn.astype(BF16)
    router_logits = jnp.einsum(
        "std,de->ste", normed_ffn, full_router, preferred_element_type=F32
    )
    router = jax.nn.softmax(router_logits, axis=-1)
    gate_prob = jnp.sum(router * chosen_float, axis=-1)
    gate_slots = jnp.sum(jnp.where(in_slot, gate_prob[..., None], 0.0), axis=1)
    gate_slots = jnp.moveaxis(gate_slots.reshape(seqs, experts, most), 0, 2).reshape(experts, slots)

    expert_in, gate_rows = to_side(to_slots(normed_ffn), gate_slots[:, None, :])
    up_parts = w_up.reshape(owned, CORES, part, model)
    down_parts = w_down.reshape(owned, CORES, part, model)
    shard = part // chips

    sets, outs, grad_ins = [], [], []
    amounts = [owned]
    for i, count in enumerate(amounts):
        first = sum(amounts[:i])
        out, grad_in, grad_up, grad_down = run_experts(
            core.astype(jnp.int32).reshape(1),
            expert_in,
            cot_rows,
            gate_rows,
            up_parts,
            down_parts,
            first,
            count,
        )
        outs.append(out)
        grad_ins.append(grad_in)
        rings = [
            Ring(grad.reshape(count, chips, shard, model), chip, forward)
            for grad, forward in ((grad_up, True), (grad_down, False))
        ]
        if i + 1 < len(amounts):
            expert_in = tie(rings, expert_in)
        sets.append((first, rings))
    total_rounds = 2 * (chips - 1)
    rounds = iter(range(total_rounds))

    def swap_held(held):
        return [[swap_cores(piece, reps) for piece in pieces] for pieces in held]

    def store(wholes, held, others, ahead):
        stored = list(wholes)
        for (first, rings), pieces, swapped in zip(sets, held, others):
            for i, (ring, piece, other) in enumerate(zip(rings, pieces, swapped)):
                for at, value in ((core, piece), (1 - core, other)):
                    stored[i] = lax.dynamic_update_slice(
                        stored[i],
                        value.astype(F32)[:, None],
                        (first, at, ring.index(ahead), 0, 0),
                    )
        return stored

    wholes = []

    def beside(stage=None, ins=()):
        step = next(rounds, None)
        if step is None:
            return stage(*ins) if stage else ()
        ins, kept = tie(sets[-1][1], (ins, list(wholes)))
        held = [[ring.held for ring in rings] for _, rings in sets]
        arrived = [[ring.move() for ring in rings] for _, rings in sets]
        if step == chips - 2:
            kept = list(fresh((owned, CORES, chips, shard, model), 2))
        if step >= chips - 1:
            others, ins = lax.optimization_barrier((swap_held(held), ins))
            kept = store(kept, held, others, chips - step)
        results = stage(*ins) if stage else ()
        arrived[0], results, kept = lax.optimization_barrier((arrived[0], results, kept))
        for (_, rings), values in zip(sets, arrived):
            for ring, value in zip(rings, values):
                ring.take(step, value)
        wholes[:] = kept
        return results

    def side_sums(outs, grad_ins):
        sums = []
        for rows in (outs, grad_ins):
            rows = jnp.concatenate(rows, axis=0)
            near = rows.shape[1] // CORES
            both = rows[:, :near].astype(F32) + swap_cores(rows[:, near:], reps).astype(F32)
            sums.append(both.astype(BF16))
        return from_side(sums[0]), sums[1]

    def to_tokens(placed):
        return jnp.einsum(
            "stc,csd->std",
            dispatch,
            placed.reshape(experts * most, seqs, model),
            preferred_element_type=F32,
        )

    cotangent = out_grad.astype(F32)

    def ffn_end(placed, grad_sums):
        grad_placed = from_side(grad_sums)
        returned = to_tokens(placed)
        layer_out = (residual + gate_prob[..., None] * returned).astype(BF16)
        grad_gate = jnp.sum(cotangent * returned, axis=-1)
        grad_logits = grad_gate[..., None] * router * (chosen_float - gate_prob[..., None])
        grad_logits = grad_logits.astype(BF16)
        grad_router = jnp.einsum("std,ste->de", normed_ffn, grad_logits, preferred_element_type=F32)
        grad_normed_ffn = to_tokens(grad_placed) + jnp.einsum(
            "ste,de->std", grad_logits, full_router, preferred_element_type=F32
        )
        grad_mid, grad_gain_ffn = rms_back(grad_normed_ffn, residual, inverse_two, gain_two)
        grad_residual = cotangent + grad_mid
        grad_attn = grad_residual.astype(BF16)
        grad_attended = jnp.einsum(
            "ste,de->std", grad_attn, full_out, preferred_element_type=F32
        ).astype(BF16)
        return layer_out, grad_router, grad_gain_ffn, grad_residual, grad_attn, grad_attended

    def scores_back(grad_attended):
        return attention_back(
            projected, grad_attended, segment_ids, seg_all, window, span, head_count
        )

    def own_keys(terms):
        if two:
            total = terms[:, :span].astype(F32) + swap_groups(terms[:, span:]).astype(F32)
            return total.astype(BF16)
        terms = jnp.roll(terms, grp_index * span, axis=1)
        return lax.psum_scatter(terms, "grp", scatter_dimension=1, tiled=True)

    def weight_grad(grad_part):
        grad = jnp.einsum("std,ste->de", normed_own, grad_part, preferred_element_type=F32)
        return grad.astype(BF16).reshape(groups, -1, model)

    def keys_end(key_terms, diagonals, grad_attn, grad_queries):
        grad_wout = jnp.einsum("std,ste->de", attended, grad_attn, preferred_element_type=F32)
        grad_wout = grad_wout.astype(BF16).reshape(groups, -1, model)
        diagonals = jnp.sum(diagonals, axis=0).reshape(head_count, groups * 2 * span)
        grad_table = jnp.einsum(
            "bo,ho->bh", bucket_hot.astype(F32), diagonals, precision=lax.Precision.HIGHEST
        )
        return own_keys(key_terms), grad_table, grad_wout, weight_grad(grad_queries)

    def halve(values, axis, place, swap):
        mine = lax.dynamic_index_in_dim(values, place, axis, keepdims=False)
        given = swap(lax.dynamic_index_in_dim(values, 1 - place, axis, keepdims=False))
        return (mine.astype(F32) + given.astype(F32)).astype(BF16)

    rows_out = model // groups
    tiny_sizes = [router_weight.size, gain_ffn.size, rel_table.size]
    tiny_cuts = np.cumsum(tiny_sizes).tolist()
    rows_tiny = -(-tiny_cuts[-1] // model)
    rows_all = 4 * rows_out + rows_tiny
    rows_all += -rows_all % (reps * 8)

    def keys_back(
        grad_keys, value_terms, far_values, grad_wq, grad_wout, grad_router, grad_gain_ffn, grad_table
    ):
        if two:
            grad_values = value_terms[:, :span].astype(F32) + far_values.astype(F32)
            grad_values = grad_values.astype(BF16)
        else:
            grad_values = own_keys(value_terms)
        tiny = (grad_router, grad_gain_ffn, grad_table)
        tiny = jnp.concatenate([value.astype(BF16).reshape(groups, -1) for value in tiny], axis=1)
        room = (rows_all - 4 * rows_out) * model - tiny.shape[1]
        tiny = jnp.pad(tiny, ((0, 0), (0, room))).reshape(groups, -1, model)
        packed = jnp.concatenate(
            [grad_wq, weight_grad(grad_keys), weight_grad(grad_values), grad_wout, tiny], axis=1
        ).reshape(groups, CORES, -1, model)
        return halve(packed, 1, core, lambda v: swap_cores(v, reps)), grad_values

    def input_back(grad_queries, grad_keys, grad_values, grad_residual):
        grad_mixed = jnp.concatenate([grad_queries, grad_keys, grad_values], axis=-1)
        grad_normed = jnp.einsum("ste,de->std", grad_mixed, full_qkv, preferred_element_type=F32)
        return grad_residual + rms_back(grad_normed, input_tokens, inverse_one, gain_one)[0]

    def group_share(parts):
        if two:
            return halve(parts, 0, grp_index, swap_groups)
        return lax.psum_scatter(parts, "grp", scatter_dimension=0, tiled=False)

    placed, grad_sums = beside(side_sums, (outs, grad_ins))
    layer_out, grad_router, grad_gain_ffn, grad_residual, grad_attn, grad_attended = beside(
        ffn_end, (placed, grad_sums)
    )
    grad_queries, key_terms, value_terms, diagonals = beside(scores_back, (grad_attended,))
    far_values = swap_groups(value_terms[:, span:]) if two else value_terms
    grad_keys, grad_table, grad_wout, grad_wq = beside(
        keys_end, (key_terms, diagonals, grad_attn, grad_queries)
    )
    parts, grad_values = beside(
        keys_back,
        (
            grad_keys,
            value_terms,
            far_values,
            grad_wq,
            grad_wout,
            grad_router,
            grad_gain_ffn,
            grad_table,
        ),
    )
    parts = beside(group_share, (parts,)).reshape(chips, -1, model)

    upward, downward = chips // 2, chips - 1 - chips // 2
    place, up_hop, down_hop = rings[0].place, rings[0].hop, rings[1].hop

    def pick(ahead):
        index = (place + ahead + chips) % chips
        return lax.dynamic_index_in_dim(parts, index, 0, keepdims=False).astype(F32)

    def put(whole, value, ahead):
        index = (place + ahead + chips) % chips
        return lax.dynamic_update_slice_in_dim(whole, value[None], index, 0)

    def reduce_stage(step):
        def stage(above, below):
            above = lax.ppermute(above, "rep", up_hop)
            if step < upward - 1:
                above = (above.astype(F32) + pick(upward - 1 - step)).astype(BF16)
            if step < downward:
                below = lax.ppermute(below, "rep", down_hop)
            if step < downward - 1:
                below = (below.astype(F32) + pick(step + 1 - downward)).astype(BF16)
            return above, below

        return stage

    def gather_stage(step):
        def stage(above, below, whole):
            above = lax.ppermute(above, "rep", up_hop)
            whole = put(whole, above, -1 - step)
            if step < downward:
                below = lax.ppermute(below, "rep", down_hop)
                whole = put(whole, below, 1 + step)
            return above, below, whole

        return stage

    above, below = pick(upward).astype(BF16), pick(-downward).astype(BF16)
    mixed = (grad_queries, grad_keys, grad_values, grad_residual)
    (above, below), tokens_grad = beside(
        lambda above, below, *mixed: (reduce_stage(0)(above, below), input_back(*mixed)),
        (above, below) + mixed,
    )
    for step in range(1, upward):
        above, below = beside(reduce_stage(step), (above, below))
    own_sum = (above.astype(F32) + below.astype(F32) + pick(0)).astype(BF16)
    above = below = own_sum
    whole = put(jnp.zeros_like(parts), own_sum, 0)
    for step in range(upward):
        above, below, whole = beside(gather_stage(step), (above, below, whole))
    whole = whole.reshape(1, -1, model)
    others = swap_cores(whole, reps)
    sums = jnp.where(
        core == 0,
        jnp.concatenate([whole, others], axis=0),
        jnp.concatenate([others, whole], axis=0),
    )
    for _ in range(total_rounds - 6 - 2 * upward):
        beside()

    sums = sums.reshape(-1, model)
    blocks = [sums[i * rows_out : (i + 1) * rows_out].astype(F32) for i in range(4)]
    tiny = sums[4 * rows_out : 4 * rows_out + rows_tiny].astype(F32).reshape(-1)
    tiny = jnp.split(tiny, tiny_cuts)
    sum_qkv = jnp.concatenate(blocks[:3], axis=1)
    sum_gain = jnp.sum(sum_qkv * query_key_value_weight.astype(F32), axis=1)
    small_sums = (
        sum_qkv,
        blocks[3],
        tiny[0].reshape(rows_out, experts),
        sum_gain / gain_attn.astype(F32),
        tiny[1],
        tiny[2].reshape(buckets // groups, head_count),
    )
    held = [[ring.held for ring in rings] for _, rings in sets]
    wholes = store(wholes, held, swap_held(held), 2 - chips)
    gathered = tuple(whole.reshape(owned * hidden, model) for whole in wholes)
    return (layer_out, tokens_grad) + small_sums + gathered


def solution(mesh):
    return jax.shard_map(
        local,
        mesh=mesh,
        in_specs=(
            P("rep", "grp", None),
            P("rep", "grp"),
            P("rep", "grp", None),
            P(),
            P("grp", None),
            P("grp", None),
            P("grp", None),
            P("grp"),
            P("grp"),
            P("grp", None),
            P("grp", None),
            P("grp", None),
            P("rep", "grp", None),
        ),
        out_specs=(
            P("rep", "grp", None),
            P("rep", "grp", None),
            P("grp", None),
            P("grp", None),
            P("grp", None),
            P("grp"),
            P("grp"),
            P("grp", None),
            P("grp", None),
            P("grp", None),
        ),
        check_vma=False,
    )
```

```python
import functools

import jax
import jax.numpy as jnp
import numpy as np
from jax import lax
from jax.experimental import pallas as pl
from jax.experimental.pallas import tpu as pltpu
from jax.sharding import PartitionSpec as P

eps_norm = 1e-06
neg_fill = -1e30
CORES = 2
PAIR = 2
F32 = jnp.float32
BF16 = jnp.bfloat16


def rms_parts(values, gain_vec):
    inverse = lax.rsqrt(jnp.mean(values * values, axis=-1, keepdims=True) + eps_norm)
    return (inverse, values * inverse * gain_vec)


def rms_back(grad_normed, values, inverse, gain_vec):
    scaled = grad_normed * gain_vec
    grad_gain = jnp.sum(grad_normed * values * inverse, axis=(0, 1))
    grad_values = inverse * (
        scaled - values * inverse * inverse * jnp.mean(scaled * values, axis=-1, keepdims=True)
    )
    return (grad_values, grad_gain)


def dot_nn(a, b):
    return lax.dot_general(a, b, (((1,), (0,)), ((), ())), preferred_element_type=F32)


def dot_nt(a, b):
    return lax.dot_general(a, b, (((1,), (1,)), ((), ())), preferred_element_type=F32)


def dot_tn(a, b):
    return lax.dot_general(a, b, (((0,), (0,)), ((), ())), preferred_element_type=F32)


def bias_tables(win_ref, table_ref, head, blocks, tile):
    width = win_ref.shape[-1]
    for b in range(blocks):
        row = win_ref[0, head * blocks + b : head * blocks + b + 1, :]
        spread = jnp.broadcast_to(row, (tile, width))
        table_ref[b] = pltpu.roll(spread, width - (tile - 1), 1, stride=1, stride_axis=0)


def bias_tile(table_ref, a, blocks, tile, span):
    start = span - tile - tile * a
    return jnp.concatenate([table_ref[b, :, start : start + span] for b in range(blocks)], axis=1)


def head_lanes(rows, width, head):
    lane = lax.broadcasted_iota(jnp.int32, (rows, width), 1)
    size = width // PAIR
    return (lane >= head * size) & (lane < (head + 1) * size)


def attention_kernel(scale, q_ref, k_ref, v_ref, seg_q_ref, seg_k_ref, win_ref, o_ref, table_ref):
    blocks, tile = table_ref.shape[0], table_ref.shape[1]
    span, width = q_ref.shape[1], q_ref.shape[2]
    keys, values = k_ref[0], v_ref[0]
    seg_keys = seg_k_ref[0]
    for head in range(PAIR):
        bias_tables(win_ref, table_ref, head, blocks, tile)
        mine = head_lanes(tile, width, head)
        for a in range(span // tile):
            rows = slice(a * tile, (a + 1) * tile)
            queries = q_ref[0, rows, :]
            queries = jnp.where(mine, queries * scale, jnp.zeros_like(queries))
            scores = dot_nt(queries, keys) + bias_tile(table_ref, a, blocks, tile, span)
            scores = jnp.where(seg_q_ref[0, rows, :] == seg_keys, scores, neg_fill)
            parts = jnp.exp(scores - jnp.max(scores, axis=1, keepdims=True))
            total = jnp.sum(parts, axis=1, keepdims=True)
            out = (dot_nn(parts.astype(BF16), values) / total).astype(BF16)
            if head == 0:
                o_ref[0, rows, :] = out
            else:
                o_ref[0, rows, :] = jnp.where(mine, out, o_ref[0, rows, :])


def attention_back_kernel(
    scale,
    q_ref,
    k_ref,
    v_ref,
    do_ref,
    seg_q_ref,
    seg_k_ref,
    win_ref,
    dq_ref,
    dk_ref,
    dv_ref,
    diag_ref,
    table_ref,
    sum_ref,
    dk_acc,
    dv_acc,
):
    blocks, tile = table_ref.shape[0], table_ref.shape[1]
    span, width = q_ref.shape[1], q_ref.shape[2]
    keys, values = k_ref[0], v_ref[0]
    seg_keys = seg_k_ref[0]
    dk_acc[...] = jnp.zeros_like(dk_acc)
    dv_acc[...] = jnp.zeros_like(dv_acc)
    for head in range(PAIR):
        bias_tables(win_ref, table_ref, head, blocks, tile)
        sum_ref[...] = jnp.zeros_like(sum_ref)
        mine = head_lanes(tile, width, head)
        for a in range(span // tile):
            rows = slice(a * tile, (a + 1) * tile)
            queries = q_ref[0, rows, :]
            queries = jnp.where(mine, queries * scale, jnp.zeros_like(queries))
            grad_out = do_ref[0, rows, :]
            grad_out = jnp.where(mine, grad_out, jnp.zeros_like(grad_out))
            scores = dot_nt(queries, keys) + bias_tile(table_ref, a, blocks, tile, span)
            scores = jnp.where(seg_q_ref[0, rows, :] == seg_keys, scores, neg_fill)
            parts = jnp.exp(scores - jnp.max(scores, axis=1, keepdims=True))
            probs = parts * (1.0 / jnp.sum(parts, axis=1, keepdims=True))
            grad_probs = dot_nt(grad_out, values)
            delta = jnp.sum(probs * grad_probs, axis=1, keepdims=True)
            wide = probs * (grad_probs - delta)
            grad_scores = wide.astype(BF16)
            dv_acc[...] += dot_tn(grad_out, probs.astype(BF16))
            dk_acc[...] += dot_tn(queries, grad_scores)
            dq = (dot_nn(grad_scores, keys) * scale.astype(np.float32)).astype(BF16)
            if head == 0:
                dq_ref[0, rows, :] = dq
            else:
                dq_ref[0, rows, :] = jnp.where(mine, dq, dq_ref[0, rows, :])
            start = span - tile - tile * a
            for b in range(blocks):
                sum_ref[b, :, start : start + span] += wide[:, b * span : (b + 1) * span]
        for b in range(blocks):
            folded = sum_ref[b]
            lanes = folded.shape[1]
            left = tile
            while left > 1:
                left //= 2
                folded = folded[:left] + pltpu.roll(folded[left:], lanes - left, 1)
            at = head * blocks + b
            diag_ref[0, 0, at : at + 1, :] = pltpu.roll(folded, tile - 1, 1)
    dk_ref[0] = dk_acc[...].T.astype(BF16)
    dv_ref[0] = dv_acc[...].T.astype(BF16)


def attention_specs(seqs, span, length, width, pairs, blocks):
    q_spec = pl.BlockSpec((1, span, width), lambda s, h: (s, 0, h))
    k_spec = pl.BlockSpec((1, length, width), lambda s, h: (s, 0, pairs + h))
    v_spec = pl.BlockSpec((1, length, width), lambda s, h: (s, 0, 2 * pairs + h))
    seg_q_spec = pl.BlockSpec((1, span, 1), lambda s, h: (s, 0, 0))
    seg_k_spec = pl.BlockSpec((1, 1, length), lambda s, h: (s, 0, 0))
    win_spec = pl.BlockSpec((1, PAIR * blocks, 2 * span), lambda s, h: (h, 0, 0))
    return q_spec, k_spec, v_spec, seg_q_spec, seg_k_spec, win_spec


def attention(projected, seg_own, seg_all, window, span, head_count):
    seqs, length, total = projected.shape
    model = total // 3
    pairs, width = head_count // PAIR, model // head_count * PAIR
    blocks = length // span
    tile = min(span, 256)
    scale = np.asarray((model // head_count) ** (-0.5), dtype=BF16)
    q_spec, k_spec, v_spec, seg_q_spec, seg_k_spec, win_spec = attention_specs(
        seqs, span, length, width, pairs, blocks
    )
    return pl.pallas_call(
        functools.partial(attention_kernel, scale),
        grid=(seqs, pairs),
        in_specs=[q_spec, k_spec, v_spec, seg_q_spec, seg_k_spec, win_spec],
        out_specs=q_spec,
        out_shape=jax.ShapeDtypeStruct((seqs, span, model), BF16),
        scratch_shapes=[pltpu.VMEM((blocks, tile, 2 * span), F32)],
        compiler_params=pltpu.CompilerParams(vmem_limit_bytes=48 * 1024 * 1024),
        cost_estimate=pl.CostEstimate(
            flops=4 * seqs * span * length * model,
            bytes_accessed=8 * seqs * length * model,
            transcendentals=seqs * head_count * span * length,
        ),
    )(projected, projected, projected, seg_own[:, :, None], seg_all[:, None, :], window)


def attention_back(projected, grad_attended, seg_own, seg_all, window, span, head_count):
    seqs, length, total = projected.shape
    model = total // 3
    pairs, width = head_count // PAIR, model // head_count * PAIR
    blocks = length // span
    tile = min(span, 256)
    scale = np.asarray((model // head_count) ** (-0.5), dtype=BF16)
    q_spec, k_spec, v_spec, seg_q_spec, seg_k_spec, win_spec = attention_specs(
        seqs, span, length, width, pairs, blocks
    )
    key_spec = pl.BlockSpec((1, length, width), lambda s, h: (s, 0, h))
    diag_spec = pl.BlockSpec((1, 1, PAIR * blocks, 2 * span), lambda s, h: (s, h, 0, 0))
    return pl.pallas_call(
        functools.partial(attention_back_kernel, scale),
        grid=(seqs, pairs),
        in_specs=[q_spec, k_spec, v_spec, q_spec, seg_q_spec, seg_k_spec, win_spec],
        out_specs=[q_spec, key_spec, key_spec, diag_spec],
        out_shape=[
            jax.ShapeDtypeStruct((seqs, span, model), BF16),
            jax.ShapeDtypeStruct((seqs, length, model), BF16),
            jax.ShapeDtypeStruct((seqs, length, model), BF16),
            jax.ShapeDtypeStruct((seqs, pairs, PAIR * blocks, 2 * span), F32),
        ],
        scratch_shapes=[
            pltpu.VMEM((blocks, tile, 2 * span), F32),
            pltpu.VMEM((blocks, tile, 2 * span), F32),
            pltpu.VMEM((width, length), F32),
            pltpu.VMEM((width, length), F32),
        ],
        compiler_params=pltpu.CompilerParams(vmem_limit_bytes=48 * 1024 * 1024),
        cost_estimate=pl.CostEstimate(
            flops=10 * seqs * span * length * model,
            bytes_accessed=16 * seqs * length * model,
            transcendentals=seqs * head_count * span * length,
        ),
    )(
        projected,
        projected,
        projected,
        grad_attended,
        seg_own[:, :, None],
        seg_all[:, None, :],
        window,
    )


def expert_kernel(
    pieces,
    core_ref,
    *refs,
):
    x_refs, cot_refs, gate_refs = (refs[i * pieces : (i + 1) * pieces] for i in range(3))
    up_ref, down_ref, out_ref, grad_in_ref, grad_up_ref, grad_down_ref = refs[3 * pieces : -4]
    rows_all, grad_out, out_acc, in_acc = refs[-4:]
    step = pl.program_id(1)

    @pl.when(step == 0)
    def _():
        start = 0
        for x_ref, cot_ref, gate_ref in zip(x_refs, cot_refs, gate_refs):
            rows = slice(start, start + x_ref.shape[1])
            start = rows.stop
            rows_all[rows, :] = x_ref[0]
            gate = jnp.broadcast_to(gate_ref[0], (128, x_ref.shape[1])).T[:, :1]
            grad_out[rows, :] = (cot_ref[0].astype(F32) * gate).astype(BF16)
        out_acc[...] = jnp.zeros_like(out_acc)
        in_acc[...] = jnp.zeros_like(in_acc)

    rows_in = rows_all[...]
    grad_rows = grad_out[...]
    up, down = up_ref[0, 0], down_ref[0, 0]
    pre = dot_nt(rows_in, up)
    grad_act = dot_nt(grad_rows, down)
    slope = np.sqrt(2.0 / np.pi).astype(np.float32)
    square = pre * pre
    tanh = jnp.tanh(slope * (pre + 0.044715 * (square * pre)))
    half = 0.5 * (1.0 + tanh)
    act = (pre * half).astype(BF16)
    inner = slope * (1.0 + (3.0 * 0.044715) * square)
    grad_pre = (grad_act * (half + (0.5 * pre) * (1.0 - tanh * tanh) * inner)).astype(BF16)
    grad_down_ref[0] = dot_tn(act, grad_rows).astype(BF16)
    grad_up_ref[0] = dot_tn(grad_pre, rows_in).astype(BF16)
    out_acc[...] += dot_nn(act, down)
    in_acc[...] += dot_nn(grad_pre, up)

    @pl.when(step == pl.num_programs(1) - 1)
    def _():
        out_ref[0] = out_acc[...].astype(BF16)
        grad_in_ref[0] = in_acc[...].astype(BF16)


def run_experts(core, rows_in, cot, gate, up, down, first, count):
    model = rows_in[0].shape[2]
    sizes = [piece.shape[1] for piece in rows_in]
    slots = sum(sizes)
    part = up.shape[2]
    fits = [t for t in (768, 512, 384, 256, 128) if part % t == 0 and slots * t <= 3 << 17]
    tile = (fits + [part])[0]
    row_specs = [pl.BlockSpec((1, n, model), lambda e, f, c: (first + e, 0, 0)) for n in sizes]
    gate_specs = [pl.BlockSpec((1, 1, n), lambda e, f, c: (first + e, 0, 0)) for n in sizes]
    weight_spec = pl.BlockSpec((1, 1, tile, model), lambda e, f, c: (first + e, c[0], f, 0))
    out_spec = pl.BlockSpec((1, slots, model), lambda e, f, c: (e, 0, 0))
    grad_spec = pl.BlockSpec((1, tile, model), lambda e, f, c: (e, f, 0))
    return pl.pallas_call(
        functools.partial(expert_kernel, len(sizes)),
        grid_spec=pltpu.PrefetchScalarGridSpec(
            num_scalar_prefetch=1,
            grid=(count, part // tile),
            in_specs=row_specs + row_specs + gate_specs + [weight_spec, weight_spec],
            out_specs=[out_spec, out_spec, grad_spec, grad_spec],
            scratch_shapes=[
                pltpu.VMEM((slots, model), BF16),
                pltpu.VMEM((slots, model), BF16),
                pltpu.VMEM((slots, model), F32),
                pltpu.VMEM((slots, model), F32),
            ],
        ),
        out_shape=[
            jax.ShapeDtypeStruct((count, slots, model), BF16),
            jax.ShapeDtypeStruct((count, slots, model), BF16),
            jax.ShapeDtypeStruct((count, part, model), BF16),
            jax.ShapeDtypeStruct((count, part, model), BF16),
        ],
        compiler_params=pltpu.CompilerParams(vmem_limit_bytes=56 * 1024 * 1024),
        cost_estimate=pl.CostEstimate(
            flops=12 * count * slots * part * model,
            bytes_accessed=8 * count * part * model,
            transcendentals=count * slots * part,
        ),
    )(core, *rows_in, *cot, *gate, up, down)


class Ring:
    def __init__(self, parts, chip, forward):
        self.parts = parts
        self.chips = chips = parts.shape[1]
        order = list(range(0, chips, 2)) + list(range(chips - 1 - chips % 2, 0, -2))
        self.place = jnp.where(chip % 2 == 0, chip // 2, chips - 1 - chip // 2)
        if not forward:
            order, self.place = order[::-1], chips - 1 - self.place
        self.hop = [
            (order[i] * CORES + c, order[(i + 1) % chips] * CORES + c)
            for i in range(chips)
            for c in range(CORES)
        ]
        self.held = self.pick(0)

    def index(self, ahead):
        return (self.place + ahead + self.chips) % self.chips

    def pick(self, ahead):
        return lax.dynamic_slice_in_dim(self.parts, self.index(ahead), 1, 1)

    def move(self):
        return lax.ppermute(self.held, "rep", self.hop)


    def take(self, step, arrived):
        if step < self.chips - 1:
            arrived = (arrived.astype(F32) + self.pick(-step - 1).astype(F32)).astype(BF16)
        self.held = arrived


def tie(rings, values):
    held, values = lax.optimization_barrier(([ring.held for ring in rings], values))
    for ring, kept in zip(rings, held):
        ring.held = kept
    return values


def fresh(shape, amount):
    return pl.pallas_call(
        lambda *refs: None,
        out_shape=[jax.ShapeDtypeStruct(shape, F32) for _ in range(amount)],
        out_specs=[pl.BlockSpec(memory_space=pl.ANY) for _ in range(amount)],
    )()


def swap_reps(values, reps, bit):
    return lax.ppermute(values, "rep", [(r, r ^ bit) for r in range(reps)])


def swap_cores(values, reps):
    return swap_reps(values, reps, 1)


def swap_groups(values):
    return lax.ppermute(values, "grp", [(0, 1), (1, 0)])


def local(
    tokens,
    segment_ids,
    expert_ids,
    rel_bucket,
    query_key_value_weight,
    output_weight,
    router_weight,
    gain_attn,
    gain_ffn,
    rel_table,
    w_up,
    w_down,
    out_grad,
):
    groups = lax.axis_size("grp")
    reps = lax.axis_size("rep")
    chips = reps // CORES
    grp_index = lax.axis_index("grp")
    rep_index = lax.axis_index("rep")
    core, chip = rep_index % CORES, rep_index // CORES
    seqs, span, model = tokens.shape
    length = span * groups
    head_count = rel_table.shape[1]
    buckets = rel_table.shape[0] * groups
    experts = router_weight.shape[1]
    owned = experts // groups
    most = span // 4
    slots = most * seqs
    hidden = w_up.shape[0] // owned
    part = hidden // CORES
    two = groups == 2

    def fetch(values):
        return swap_groups(values) if two else lax.all_gather(values, "grp", axis=0)

    def rotated(values, fetched, axis):
        if two:
            return jnp.concatenate([values, fetched], axis=axis)
        whole = jnp.concatenate([fetched[i] for i in range(groups)], axis=axis)
        return jnp.roll(whole, -grp_index * values.shape[axis], axis=axis)

    def stacked(values, fetched):
        if not two:
            return fetched
        return jnp.where(
            grp_index == 0, jnp.stack([values, fetched]), jnp.stack([fetched, values])
        )

    def gather_weight(values, after):
        if not two:
            return lax.all_gather(values, "grp", axis=0, tiled=True), after
        rows = values.shape[0]
        sharers = 4 if reps % 4 == 0 and rows % 64 == 0 else 2
        piece = rows // sharers
        place = rep_index % sharers
        pieces = {0: swap_groups(lax.dynamic_slice_in_dim(values, place * piece, piece, 0))}
        if sharers == 4:
            pieces[2] = swap_reps(pieces[0], reps, 2)
            pieces[2], after = lax.optimization_barrier((pieces[2], after))
        for bit in list(pieces):
            pieces[bit | 1] = swap_cores(pieces[bit], reps)
        whole = jnp.zeros((2 * rows,) + values.shape[1:], values.dtype)
        whole = lax.dynamic_update_slice_in_dim(whole, values, grp_index * rows, 0)
        start = (1 - grp_index) * rows
        for bit, fetched in pieces.items():
            whole = lax.dynamic_update_slice_in_dim(
                whole, fetched, start + (place ^ bit) * piece, 0
            )
        return whole, after

    def gather_whole(values):
        if not two:
            return lax.all_gather(values, "grp", axis=0, tiled=True)
        rows = values.shape[0]
        whole = jnp.zeros((2 * rows,) + values.shape[1:], values.dtype)
        whole = lax.dynamic_update_slice_in_dim(whole, values, grp_index * rows, 0)
        return lax.dynamic_update_slice_in_dim(
            whole, swap_groups(values), (1 - grp_index) * rows, 0
        )

    small = jnp.concatenate(
        [router_weight.reshape(-1), gain_attn, gain_ffn, rel_table.reshape(-1)]
    )
    small_far, tokens_far = fetch(small), fetch(tokens)
    full_qkv, (small_far, tokens_far) = gather_weight(
        query_key_value_weight, (small_far, tokens_far)
    )
    small = stacked(small, small_far)
    cuts = np.cumsum([router_weight.size, gain_attn.size, gain_ffn.size]).tolist()
    full_router, full_gain_attn, full_gain_ffn, full_table = jnp.split(small, cuts, axis=1)
    full_router = full_router.reshape(model, experts)
    full_table = full_table.reshape(buckets, head_count)
    gain_one = full_gain_attn.reshape(-1).astype(F32)
    gain_two = full_gain_ffn.reshape(-1).astype(F32)
    tokens_far, late_out, late_ids = lax.optimization_barrier(
        (tokens_far, output_weight, segment_ids)
    )
    tokens_all = rotated(tokens, tokens_far, 1)
    ids_far, late_out = lax.optimization_barrier((fetch(late_ids), late_out))
    seg_all = rotated(late_ids, ids_far, 1)
    full_out = gather_whole(late_out)

    first_expert = grp_index * owned if two else 0
    expert_of = expert_ids[..., 0]
    chosen = expert_of[..., None] == jnp.arange(experts)
    chosen_float = chosen.astype(F32)
    strict_lower = (jnp.arange(span)[:, None] > jnp.arange(span)[None, :]).astype(BF16)
    earlier = jnp.einsum("tu,sue->ste", strict_lower, chosen.astype(BF16), preferred_element_type=F32)
    slot_rank = jnp.sum(earlier * chosen_float, axis=-1).astype(jnp.int32)
    slot_index = (expert_of - first_expert + experts) % experts * most + slot_rank
    in_slot = slot_index[..., None] == jnp.arange(experts * most)
    dispatch = in_slot.astype(BF16)

    def to_slots(rows):
        parts = jnp.split(dispatch, 2, axis=2) if two else [dispatch]
        placed = [
            jnp.einsum("stc,std->csd", part, rows, preferred_element_type=F32) for part in parts
        ]
        return [value.astype(BF16).reshape(-1, slots, model) for value in placed]

    def to_side(parts):
        if two:
            return [parts[0], swap_groups(parts[1])]
        split = parts[0].reshape((groups, owned) + parts[0].shape[1:])
        moved = lax.all_to_all(split, "grp", 0, 0, tiled=False)
        return [moved[i] for i in range(groups)]

    def to_cores(pieces):
        return pieces + [swap_cores(piece, reps) for piece in pieces]

    def from_side(rows):
        if two:
            return jnp.concatenate([rows[:, :slots], swap_groups(rows[:, slots:])], axis=0)
        moved = jnp.moveaxis(rows.reshape(owned, groups, slots, model), 1, 0)
        return lax.all_to_all(moved, "grp", 0, 0, tiled=False).reshape(experts, slots, model)

    input_tokens = tokens.astype(F32)
    inverse_one, normed_own = rms_parts(input_tokens, gain_one)
    normed_own = normed_own.astype(BF16)
    normed_all = rms_parts(tokens_all.astype(F32), gain_one)[1].astype(BF16)
    projected = jnp.einsum(
        "std,de->ste", normed_all, full_qkv, preferred_element_type=F32
    ).astype(BF16)

    projected, full_out, cot_slots = lax.optimization_barrier(
        (projected, full_out, to_slots(out_grad))
    )
    cot_rows = to_side(cot_slots)

    bucket_line = jnp.pad(rel_bucket, (0, 1), constant_values=buckets)
    starts = [
        ((grp_index + b) % groups - grp_index) * span + length - span for b in range(groups)
    ]
    bucket_window = jnp.stack(
        [lax.dynamic_slice_in_dim(bucket_line, at, 2 * span, 0) for at in starts]
    )
    bucket_hot = bucket_window[None] == jnp.arange(buckets)[:, None, None]
    bucket_hot = bucket_hot.reshape(buckets, groups * 2 * span)
    window = jnp.einsum(
        "bh,bo->ho", full_table, bucket_hot.astype(BF16), preferred_element_type=F32
    ).reshape(head_count // PAIR, PAIR * groups, 2 * span)

    attended = attention(projected, segment_ids, seg_all, window, span, head_count)
    attended, cot_rows = lax.optimization_barrier((attended, cot_rows))
    cot_rows = to_cores(cot_rows)
    residual = input_tokens + jnp.einsum(
        "std,de->ste", attended, full_out, preferred_element_type=F32
    )
    inverse_two, normed_ffn = rms_parts(residual, gain_two)
    normed_ffn = normed_ffn.astype(BF16)
    router_logits = jnp.einsum(
        "std,de->ste", normed_ffn, full_router, preferred_element_type=F32
    )
    router = jax.nn.softmax(router_logits, axis=-1)
    gate_prob = jnp.sum(router * chosen_float, axis=-1)
    gate_slots = jnp.sum(jnp.where(in_slot, gate_prob[..., None], 0.0), axis=1)
    gate_slots = jnp.moveaxis(gate_slots.reshape(seqs, experts, most), 0, 2).reshape(experts, slots)

    gate_parts = jnp.split(gate_slots[:, None, :], groups if two else 1)
    expert_in, gate_rows = lax.optimization_barrier(
        (to_side(to_slots(normed_ffn)), to_side(gate_parts))
    )
    expert_in, gate_rows = to_cores(expert_in), to_cores(gate_rows)
    up_parts = w_up.reshape(owned, CORES, part, model)
    down_parts = w_down.reshape(owned, CORES, part, model)
    shard = part // chips

    sets, outs, grad_ins = [], [], []
    amounts = [owned]
    for i, count in enumerate(amounts):
        first = sum(amounts[:i])
        out, grad_in, grad_up, grad_down = run_experts(
            core.astype(jnp.int32).reshape(1),
            expert_in,
            cot_rows,
            gate_rows,
            up_parts,
            down_parts,
            first,
            count,
        )
        outs.append(out)
        grad_ins.append(grad_in)
        rings = [
            Ring(grad.reshape(count, chips, shard, model), chip, forward)
            for grad, forward in ((grad_up, True), (grad_down, False))
        ]
        if i + 1 < len(amounts):
            expert_in = tie(rings, expert_in)
        sets.append((first, rings))
    total_rounds = 2 * (chips - 1)
    rounds = iter(range(total_rounds))

    def swap_held(held):
        return [[swap_cores(piece, reps) for piece in pieces] for pieces in held]

    def store(wholes, held, others, ahead):
        stored = list(wholes)
        for (first, rings), pieces, swapped in zip(sets, held, others):
            for i, (ring, piece, other) in enumerate(zip(rings, pieces, swapped)):
                for at, value in ((core, piece), (1 - core, other)):
                    stored[i] = lax.dynamic_update_slice(
                        stored[i],
                        value.astype(F32)[:, None],
                        (first, at, ring.index(ahead), 0, 0),
                    )
        return stored

    wholes = []

    def beside(stage=None, ins=()):
        step = next(rounds, None)
        if step is None:
            return stage(*ins) if stage else ()
        ins, kept = tie(sets[-1][1], (ins, list(wholes)))
        held = [[ring.held for ring in rings] for _, rings in sets]
        arrived = [[ring.move() for ring in rings] for _, rings in sets]
        if step == chips - 2:
            kept = list(fresh((owned, CORES, chips, shard, model), 2))
        if step >= chips - 1:
            others, ins = lax.optimization_barrier((swap_held(held), ins))
            kept = store(kept, held, others, chips - step)
        results = stage(*ins) if stage else ()
        arrived[0], results, kept = lax.optimization_barrier((arrived[0], results, kept))
        for (_, rings), values in zip(sets, arrived):
            for ring, value in zip(rings, values):
                ring.take(step, value)
        wholes[:] = kept
        return results

    def side_sums(outs, grad_ins):
        sums = []
        for rows in (outs, grad_ins):
            rows = jnp.concatenate(rows, axis=0)
            near = rows.shape[1] // CORES
            both = rows[:, :near].astype(F32) + swap_cores(rows[:, near:], reps).astype(F32)
            sums.append(both.astype(BF16))
        return from_side(sums[0]), sums[1]

    def to_tokens(placed):
        return jnp.einsum(
            "stc,csd->std",
            dispatch,
            placed.reshape(experts * most, seqs, model),
            preferred_element_type=F32,
        )

    cotangent = out_grad.astype(F32)

    def ffn_end(placed, grad_sums):
        grad_placed = from_side(grad_sums)
        returned = to_tokens(placed)
        layer_out = (residual + gate_prob[..., None] * returned).astype(BF16)
        grad_gate = jnp.sum(cotangent * returned, axis=-1)
        grad_logits = grad_gate[..., None] * router * (chosen_float - gate_prob[..., None])
        grad_logits = grad_logits.astype(BF16)
        grad_router = jnp.einsum("std,ste->de", normed_ffn, grad_logits, preferred_element_type=F32)
        grad_normed_ffn = to_tokens(grad_placed) + jnp.einsum(
            "ste,de->std", grad_logits, full_router, preferred_element_type=F32
        )
        grad_mid, grad_gain_ffn = rms_back(grad_normed_ffn, residual, inverse_two, gain_two)
        grad_residual = cotangent + grad_mid
        grad_attn = grad_residual.astype(BF16)
        grad_attended = jnp.einsum(
            "ste,de->std", grad_attn, full_out, preferred_element_type=F32
        ).astype(BF16)
        return layer_out, grad_router, grad_gain_ffn, grad_residual, grad_attn, grad_attended

    def scores_back(grad_attended):
        return attention_back(
            projected, grad_attended, segment_ids, seg_all, window, span, head_count
        )

    def own_keys(terms):
        if two:
            total = terms[:, :span].astype(F32) + swap_groups(terms[:, span:]).astype(F32)
            return total.astype(BF16)
        terms = jnp.roll(terms, grp_index * span, axis=1)
        return lax.psum_scatter(terms, "grp", scatter_dimension=1, tiled=True)

    def weight_grad(grad_part):
        grad = jnp.einsum("std,ste->de", normed_own, grad_part, preferred_element_type=F32)
        return grad.astype(BF16).reshape(groups, -1, model)

    def keys_end(key_terms, diagonals, grad_attn, grad_queries):
        grad_wout = jnp.einsum("std,ste->de", attended, grad_attn, preferred_element_type=F32)
        grad_wout = grad_wout.astype(BF16).reshape(groups, -1, model)
        diagonals = jnp.sum(diagonals, axis=0).reshape(head_count, groups * 2 * span)
        grad_table = jnp.einsum(
            "bo,ho->bh", bucket_hot.astype(F32), diagonals, precision=lax.Precision.HIGHEST
        )
        return own_keys(key_terms), grad_table, grad_wout, weight_grad(grad_queries)

    def halve(values, axis, place, swap):
        mine = lax.dynamic_index_in_dim(values, place, axis, keepdims=False)
        given = swap(lax.dynamic_index_in_dim(values, 1 - place, axis, keepdims=False))
        return (mine.astype(F32) + given.astype(F32)).astype(BF16)

    rows_out = model // groups
    tiny_sizes = [router_weight.size, gain_ffn.size, rel_table.size]
    tiny_cuts = np.cumsum(tiny_sizes).tolist()
    rows_tiny = -(-tiny_cuts[-1] // model)
    rows_all = 4 * rows_out + rows_tiny
    rows_all += -rows_all % (reps * 8)

    def keys_back(
        grad_keys, value_terms, far_values, grad_wq, grad_wout, grad_router, grad_gain_ffn, grad_table
    ):
        if two:
            grad_values = value_terms[:, :span].astype(F32) + far_values.astype(F32)
            grad_values = grad_values.astype(BF16)
        else:
            grad_values = own_keys(value_terms)
        tiny = (grad_router, grad_gain_ffn, grad_table)
        tiny = jnp.concatenate([value.astype(BF16).reshape(groups, -1) for value in tiny], axis=1)
        room = (rows_all - 4 * rows_out) * model - tiny.shape[1]
        tiny = jnp.pad(tiny, ((0, 0), (0, room))).reshape(groups, -1, model)
        packed = jnp.concatenate(
            [grad_wq, weight_grad(grad_keys), weight_grad(grad_values), grad_wout, tiny], axis=1
        ).reshape(groups, CORES, -1, model)
        return halve(packed, 1, core, lambda v: swap_cores(v, reps)), grad_values

    def input_back(grad_queries, grad_keys, grad_values, grad_residual):
        grad_mixed = jnp.concatenate([grad_queries, grad_keys, grad_values], axis=-1)
        grad_normed = jnp.einsum("ste,de->std", grad_mixed, full_qkv, preferred_element_type=F32)
        return grad_residual + rms_back(grad_normed, input_tokens, inverse_one, gain_one)[0]

    def group_share(parts):
        if two:
            return halve(parts, 0, grp_index, swap_groups)
        return lax.psum_scatter(parts, "grp", scatter_dimension=0, tiled=False)

    placed, grad_sums = beside(side_sums, (outs, grad_ins))
    layer_out, grad_router, grad_gain_ffn, grad_residual, grad_attn, grad_attended = beside(
        ffn_end, (placed, grad_sums)
    )
    grad_queries, key_terms, value_terms, diagonals = beside(scores_back, (grad_attended,))
    far_values = swap_groups(value_terms[:, span:]) if two else value_terms
    grad_keys, grad_table, grad_wout, grad_wq = beside(
        keys_end, (key_terms, diagonals, grad_attn, grad_queries)
    )
    parts, grad_values = beside(
        keys_back,
        (
            grad_keys,
            value_terms,
            far_values,
            grad_wq,
            grad_wout,
            grad_router,
            grad_gain_ffn,
            grad_table,
        ),
    )
    parts = beside(group_share, (parts,)).reshape(chips, -1, model)

    upward, downward = chips // 2, chips - 1 - chips // 2
    place, up_hop, down_hop = rings[0].place, rings[0].hop, rings[1].hop

    def pick(ahead):
        index = (place + ahead + chips) % chips
        return lax.dynamic_index_in_dim(parts, index, 0, keepdims=False).astype(F32)

    def put(whole, value, ahead):
        index = (place + ahead + chips) % chips
        return lax.dynamic_update_slice_in_dim(whole, value[None], index, 0)

    def reduce_stage(step):
        def stage(above, below):
            above = lax.ppermute(above, "rep", up_hop)
            if step < upward - 1:
                above = (above.astype(F32) + pick(upward - 1 - step)).astype(BF16)
            if step < downward:
                below = lax.ppermute(below, "rep", down_hop)
            if step < downward - 1:
                below = (below.astype(F32) + pick(step + 1 - downward)).astype(BF16)
            return above, below

        return stage

    def gather_stage(step):
        def stage(above, below, whole):
            above = lax.ppermute(above, "rep", up_hop)
            whole = put(whole, above, -1 - step)
            if step < downward:
                below = lax.ppermute(below, "rep", down_hop)
                whole = put(whole, below, 1 + step)
            return above, below, whole

        return stage

    above, below = pick(upward).astype(BF16), pick(-downward).astype(BF16)
    mixed = (grad_queries, grad_keys, grad_values, grad_residual)
    (above, below), tokens_grad = beside(
        lambda above, below, *mixed: (reduce_stage(0)(above, below), input_back(*mixed)),
        (above, below) + mixed,
    )
    for step in range(1, upward):
        above, below = beside(reduce_stage(step), (above, below))
    own_sum = (above.astype(F32) + below.astype(F32) + pick(0)).astype(BF16)
    above = below = own_sum
    whole = put(jnp.zeros_like(parts), own_sum, 0)
    for step in range(upward):
        above, below, whole = beside(gather_stage(step), (above, below, whole))
    whole = whole.reshape(1, -1, model)
    others = swap_cores(whole, reps)
    sums = jnp.where(
        core == 0,
        jnp.concatenate([whole, others], axis=0),
        jnp.concatenate([others, whole], axis=0),
    )
    for _ in range(total_rounds - 6 - 2 * upward):
        beside()

    sums = sums.reshape(-1, model)
    blocks = [sums[i * rows_out : (i + 1) * rows_out].astype(F32) for i in range(4)]
    tiny = sums[4 * rows_out : 4 * rows_out + rows_tiny].astype(F32).reshape(-1)
    tiny = jnp.split(tiny, tiny_cuts)
    sum_qkv = jnp.concatenate(blocks[:3], axis=1)
    sum_gain = jnp.sum(sum_qkv * query_key_value_weight.astype(F32), axis=1)
    small_sums = (
        sum_qkv,
        blocks[3],
        tiny[0].reshape(rows_out, experts),
        sum_gain / gain_attn.astype(F32),
        tiny[1],
        tiny[2].reshape(buckets // groups, head_count),
    )
    held = [[ring.held for ring in rings] for _, rings in sets]
    wholes = store(wholes, held, swap_held(held), 2 - chips)
    gathered = tuple(whole.reshape(owned * hidden, model) for whole in wholes)
    return (layer_out, tokens_grad) + small_sums + gathered


def solution(mesh):
    return jax.shard_map(
        local,
        mesh=mesh,
        in_specs=(
            P("rep", "grp", None),
            P("rep", "grp"),
            P("rep", "grp", None),
            P(),
            P("grp", None),
            P("grp", None),
            P("grp", None),
            P("grp"),
            P("grp"),
            P("grp", None),
            P("grp", None),
            P("grp", None),
            P("rep", "grp", None),
        ),
        out_specs=(
            P("rep", "grp", None),
            P("rep", "grp", None),
            P("grp", None),
            P("grp", None),
            P("grp", None),
            P("grp"),
            P("grp"),
            P("grp", None),
            P("grp", None),
            P("grp", None),
        ),
        check_vma=False,
    )
```
